32 devices in a mesh: tok: 8 (over z, y), ffn: 4 (over x, core).
Axes of the slice: x: 2, y: 2, z: 4, core: 2. Of those that a mesh axis runs over, the one named last changes fastest.
Arguments:
- enc_in: bfloat16 [5120, 768], P(('tok', 'ffn')), may hold values from -6 to 6
- dec_in: bfloat16 [5120, 768], P(('tok', 'ffn')), may hold values from -6 to 6
- cotangent: bfloat16 [5120, 768], P(('tok', 'ffn')), may hold values from -6 to 6
- enc_lengths: int32 [8, 5], P('tok'), may hold values from 1 to 512, 640 in all within a row
- dec_lengths: int32 [8, 5], P('tok'), may hold values from 16 to 114, as said below
- qk_weights: bfloat16 [3, 2, 768, 768], replicated, may hold values from -0.109375 to 0.109375
- v_weights: bfloat16 [3, 768, 768], replicated, may hold values from -0.21875 to 0.21875
- out_weights: bfloat16 [3, 768, 768], replicated, may hold values from -0.875 to 0.875
- ffn_in: bfloat16 [2, 768, 3072], P(None, None, 'ffn'), may hold values from -0.21875 to 0.21875
- ffn_out: bfloat16 [2, 3072, 768], P(None, 'ffn'), may hold values from -0.15625 to 0.15625
- bias_tables: float32 [2, 32, 12], replicated, may hold values from -4 to 4
- gains: float32 [6, 768], replicated, may hold values from 0.5 to 1.5
Outputs:
- dec_out: bfloat16 [5120, 768], P(('tok', 'ffn'))
- enc_grad: bfloat16 [5120, 768], P(('tok', 'ffn'))
- dec_grad: bfloat16 [5120, 768], P(('tok', 'ffn'))
- qk_grads: float32 [3, 2, 768, 768], P(None, None, 'tok', 'ffn')
- v_grads: float32 [3, 768, 768], P(None, 'tok', 'ffn')
- out_grads: float32 [3, 768, 768], P(None, 'ffn', 'tok')
- ffn_in_grads: float32 [2, 768, 3072], P(None, 'tok', 'ffn')
- ffn_out_grads: float32 [2, 3072, 768], P(None, 'ffn', 'tok')
- table_grads: float32 [2, 32, 12], replicated
- gain_grads: float32 [6, 768], replicated
- final_gain_grad: float32 [768], replicated
The draws below stay inside these ranges and needn't reach their ends.
Inputs may be any that keep to these rules, and one draw needn't show every extreme that they name: `enc_lengths`: in each pack the 5 example lengths sum to 640, and the longest is exactly 512. `dec_lengths`: in each pack one example's target has exactly 114 tokens.
All inputs are finite; a program needn't handle non-finite values.
Results may differ from the reference program's by a relative error of at most 0.028.
Values may be sent and summed in bfloat16 or wider, within the bound.
A program may use at most 320 MiB of HBM per device.

```python
import math
import jax
import jax.numpy as jnp
import numpy as np
from jax import lax

D = 768
H = 12
DH = 64
FF = 3072
BUCKETS = 32
EX = 5
SLOT = 128
LONGEST = 512
TARGET_MIN = 16
TARGET_MAX = 114
HD = 768
PACK = 640
PACKS = 8
TOKENS = 5120


def draw_dec_lengths(key, part):
    first_key, second_key = jax.random.split(jax.random.fold_in(key, 11))
    lengths = jax.random.randint(first_key, (PACKS, EX), TARGET_MIN, TARGET_MAX + 1, dtype=jnp.int32)
    longest = jax.random.randint(second_key, (PACKS, 1), 0, EX, dtype=jnp.int32)
    column = jnp.arange(EX, dtype=jnp.int32)[None, :]
    return jnp.where(column == longest, TARGET_MAX, lengths).astype(jnp.int32)


def with_spikes(entries, own_key, source, target, parts, factor):
    def block_of(dim):
        return (jnp.arange(entries.shape[dim]) // (entries.shape[dim] // parts)).reshape((-1,) + (1,) * (entries.ndim - 1 - dim))

    first = jax.random.permutation(own_key, parts)[block_of(target)]
    second = (block_of(target) + parts // 2) % parts
    return jnp.where((block_of(source) == first) | (block_of(source) == second), factor * entries, entries)


def level_of(own_key, shape, shards, least, high):
    level = 1.0
    for axis_at, parts in shards:
        steps = jax.random.uniform(jax.random.fold_in(jax.random.fold_in(own_key, 6), axis_at), (parts,), jnp.float32, least / len(shards), high / len(shards))
        level = level * jnp.repeat(jnp.exp(steps), shape[axis_at] // parts).reshape((-1,) + (1,) * (len(shape) - 1 - axis_at))
    return level


def profile(number_of, total, limit, skew):
    loads = [(1 << 20) // math.isqrt(rank ** skew) + 1 for rank in range(2, number_of + 1)]
    rest, holding = total - limit - (number_of - 1), [1] * (number_of - 1)
    while rest > 0:
        free = [i for i in range(number_of - 1) if holding[i] < limit]
        whole, left = sum([loads[i] for i in free]), rest
        for i in free:
            addition = min(limit - holding[i], max(1, left * loads[i] // whole), rest)
            holding[i] = holding[i] + addition
            rest = rest - addition
    return np.array([limit] + holding)


def uneven_parts(key, amount, total, bound, skew):
    if amount == 2:
        one = jax.random.randint(key, (), max(1, total - bound), min(bound, total - 1) + 1)
        return jnp.stack([one, total - one])
    sizes = jnp.asarray(profile(amount, total, bound, skew), jnp.int32)
    twos = (amount - 1) // 2
    source_of, receiver = sizes[1:1 + 2 * twos:2], sizes[2:2 + 2 * twos:2]
    room = jnp.minimum(source_of - 1, bound - receiver)
    moved = jax.random.randint(jax.random.fold_in(key, 1), (twos,), 0, 1 << 20) % (room + 1)
    sizes = sizes.at[1:1 + 2 * twos:2].set(source_of - moved).at[2:2 + 2 * twos:2].set(receiver + moved)
    return sizes[jax.random.permutation(jax.random.fold_in(key, 2), amount)]


def centred(own_key, dims, width, limit, cuts=(), held_as=jnp.bfloat16):
    values = jax.random.normal(own_key, dims, jnp.float32) * width
    if len(cuts) > 0:
        values = level_of(own_key, dims, cuts, -0.22, 0.18) * values
    return jnp.clip(values, min=-limit, max=limit).astype(held_as)


def heavy_noise(key, dims, scale, bound, cuts, heavy, kind=jnp.bfloat16):
    drawn = scale * jax.random.normal(key, dims, jnp.float32)
    if cuts:
        drawn = drawn * level_of(key, dims, cuts, -0.22, 0.18)
    return jnp.clip(with_spikes(drawn, jax.random.fold_in(key, 3), *heavy), -bound, bound).astype(kind)


def setup_inputs(seed: int = 0) -> dict:
    streams_of = jax.random.split(jax.random.key(seed), 13)
    enc_in = heavy_noise(streams_of[0], (TOKENS, D), 1.0, 6.0, ((0, 32),), (0, 1, 32, 2.75))
    dec_in = heavy_noise(streams_of[1], (TOKENS, D), 1.0, 6.0, ((0, 32),), (0, 1, 32, 2.75))
    cotangent = heavy_noise(streams_of[2], (TOKENS, D), 1.0, 6.0, ((0, 32),), (0, 1, 32, 2.75))
    enc_lengths = jax.vmap(lambda own: uneven_parts(own, EX, PACK, LONGEST, 2))(jax.random.split(streams_of[3], PACKS)).reshape((PACKS, EX)).astype(jnp.int32)
    dec_lengths = draw_dec_lengths(jax.random.fold_in(streams_of[12], 71), 0)
    qk_weights = centred(streams_of[5], (3, 2, D, HD), (4 * D) ** -0.5, 0.109375)
    v_weights = centred(streams_of[6], (3, D, HD), D ** -0.5, 0.21875)
    out_weights = centred(streams_of[7], (3, HD, D), (HD // 16) ** -0.5, 0.875)
    ffn_in = centred(streams_of[8], (2, D, FF), D ** -0.5, 0.21875, ((2, 4),))
    ffn_out = centred(streams_of[9], (2, FF, D), (FF // 2) ** -0.5, 0.15625, ((1, 4),))
    bias_tables = centred(streams_of[10], (2, BUCKETS, H), 1.0, 4.0, (), jnp.float32)
    gains = jnp.clip(1.0 + 0.1 * jax.random.normal(streams_of[11], (6, D), jnp.float32), 0.5, 1.5)
    return {"enc_in": enc_in, "dec_in": dec_in, "cotangent": cotangent, "enc_lengths": enc_lengths, "dec_lengths": dec_lengths, "qk_weights": qk_weights, "v_weights": v_weights, "out_weights": out_weights, "ffn_in": ffn_in, "ffn_out": ffn_out, "bias_tables": bias_tables, "gains": gains}


norm_epsilon = 1e-06
masked_score = -1000000000.0
wide_limits = (12, 16, 23, 32, 46, 64, 91)
causal_limits = (19, 21, 24, 27, 31, 35, 40, 46, 52, 59, 67, 77, 87, 99, 113)

@jax.custom_vjp
def low(v):
    return lax.optimization_barrier(v.astype(jnp.bfloat16)).astype(jnp.float32)

@jax.custom_vjp
def low_back(v):
    return v

def low_keep(v):
    return (low(v), None)

def low_pass(kept, grad):
    return (grad,)

def back_keep(v):
    return (v, None)

def back_low(kept, grad):
    return (low(grad),)
low.defvjp(low_keep, low_pass)
low_back.defvjp(back_keep, back_low)

def bucket_index(relative, causal):
    if causal:
        distance = jnp.maximum(-relative, 0)
        limits = jnp.array(causal_limits, dtype=jnp.int32)
        far = 16 + lax.optimization_barrier(jnp.sum((distance[..., None] >= limits).astype(jnp.int32), axis=-1)).astype(jnp.int32)
        return jnp.where(distance < 16, distance, far).astype(jnp.int32)
    distance = jnp.abs(relative)
    limits = jnp.array(wide_limits, dtype=jnp.int32)
    far = 8 + lax.optimization_barrier(jnp.sum((distance[..., None] >= limits).astype(jnp.int32), axis=-1)).astype(jnp.int32)
    return (jnp.where(distance < 8, distance, far) + 16 * (relative > 0).astype(jnp.int32)).astype(jnp.int32)

def matmul(left, right):
    return jnp.dot(left, right, precision=lax.Precision.HIGHEST)

def rms_scale(values, gain_vector):
    return values * lax.rsqrt(lax.optimization_barrier(jnp.mean(values * values, axis=-1, keepdims=True)) + norm_epsilon) * gain_vector

def attention(source_q, source_kv, w_query, w_key, w_value, w_out, bias, live_mask):
    query = low_back(low(matmul(source_q, w_query))).reshape(source_q.shape[0], H, DH)
    key_proj = low_back(low(matmul(source_kv, w_key))).reshape(source_kv.shape[0], H, DH)
    value_proj = low_back(low(matmul(source_kv, w_value))).reshape(source_kv.shape[0], H, DH)
    scores = jnp.einsum('qhd,khd->hqk', query, key_proj, precision=lax.Precision.HIGHEST)
    if bias is not None:
        scores = scores + bias
    scores = low_back(scores)
    weights = low(jax.nn.softmax(jnp.where(live_mask[None], scores, masked_score), axis=-1))
    mixed = jnp.einsum('hqk,khd->qhd', weights, value_proj, precision=lax.Precision.HIGHEST)
    mixed = low_back(low(mixed.reshape(source_q.shape[0], H * DH)))
    return low_back(matmul(mixed, w_out))

def feed_forward(normed, w_in, w_out):
    pre = low_back(matmul(normed, w_in))
    hidden = low_back(low(jax.nn.gelu(pre, approximate=False)))
    return low_back(matmul(hidden, w_out))

def pack_forward(params, enc_pack, dec_pack, enc_len, dec_len):
    qk_w, value_w, out_w, in_w, down_w, tables, gain_rows = params
    positions = jnp.arange(PACK, dtype=jnp.int32)
    example_ends = jnp.cumsum(enc_len).astype(jnp.int32)
    example_starts = (example_ends - enc_len).astype(jnp.int32)
    enc_segment = lax.optimization_barrier(jnp.sum((positions[:, None] >= example_starts[None, :]).astype(jnp.int32), axis=1)).astype(jnp.int32) - 1
    dec_segment = (positions // SLOT).astype(jnp.int32)
    slot_length = jnp.take(dec_len, dec_segment)
    dec_valid = positions % SLOT < slot_length
    relative = (positions[None, :] - positions[:, None]).astype(jnp.int32)
    enc_bias = jnp.transpose(jnp.take(tables[0], bucket_index(relative, False), axis=0), (2, 0, 1))
    dec_bias = jnp.transpose(jnp.take(tables[1], bucket_index(relative, True), axis=0), (2, 0, 1))
    enc_live = enc_segment[:, None] == enc_segment[None, :]
    self_live = (dec_segment[:, None] == dec_segment[None, :]) & (relative <= 0) & dec_valid[None, :]
    cross_live = dec_segment[:, None] == enc_segment[None, :]
    normed_a = low(rms_scale(enc_pack, gain_rows[0]))
    enc_mid = enc_pack + attention(normed_a, normed_a, qk_w[0, 0], qk_w[0, 1], value_w[0], out_w[0], enc_bias, enc_live)
    normed_b = low(rms_scale(enc_mid, gain_rows[1]))
    enc_last = enc_mid + feed_forward(normed_b, in_w[0], down_w[0])
    memory = low(rms_scale(enc_last, gain_rows[2]))
    normed_c = low(rms_scale(dec_pack, gain_rows[3]))
    dec_first = dec_pack + attention(normed_c, normed_c, qk_w[1, 0], qk_w[1, 1], value_w[1], out_w[1], dec_bias, self_live)
    normed_d = low(rms_scale(dec_first, gain_rows[4]))
    dec_second = dec_first + attention(normed_d, memory, qk_w[2, 0], qk_w[2, 1], value_w[2], out_w[2], None, cross_live)
    normed_e = low(rms_scale(dec_second, gain_rows[5]))
    return dec_second + feed_forward(normed_e, in_w[1], down_w[1])

def reference(enc_in, dec_in, cotangent, enc_lengths, dec_lengths, qk_weights, v_weights, out_weights, ffn_in, ffn_out, bias_tables, gains):
    params = (qk_weights.astype(jnp.float32), v_weights.astype(jnp.float32), out_weights.astype(jnp.float32), ffn_in.astype(jnp.float32), ffn_out.astype(jnp.float32), bias_tables.astype(jnp.float32), gains.astype(jnp.float32))
    enc_packs = enc_in.astype(jnp.float32).reshape(PACKS, PACK, D)
    dec_packs = dec_in.astype(jnp.float32).reshape(PACKS, PACK, D)

    def forward(weights_all, enc_all, dec_all):

        def one_pack(pieces):
            return pack_forward(weights_all, pieces[0], pieces[1], pieces[2], pieces[3])
        return lax.map(jax.checkpoint(one_pack), (enc_all, dec_all, enc_lengths, dec_lengths))
    dec_final, pull_back = jax.vjp(forward, params, enc_packs, dec_packs)
    weight_grads, enc_back, dec_back = pull_back(cotangent.astype(jnp.float32).reshape(PACKS, PACK, D))
    return (dec_final.reshape(PACKS * PACK, D).astype(jnp.bfloat16), enc_back.reshape(PACKS * PACK, D).astype(jnp.bfloat16), dec_back.reshape(PACKS * PACK, D).astype(jnp.bfloat16), weight_grads[0], weight_grads[1], weight_grads[2], weight_grads[3], weight_grads[4], weight_grads[5], weight_grads[6], weight_grads[6][5])
```

```python
import functools
import jax
import jax.numpy as jnp
from jax import lax
from jax.experimental import pallas as pl
from jax.experimental.pallas import tpu as pltpu
from jax.sharding import PartitionSpec as P

DH = 64
BUCKETS = 32
SLOT = 128
GROUP = 4
BF = jnp.bfloat16
F32 = jnp.float32
MESH = pl.DeviceIdType.MESH

norm_epsilon = 1e-06
masked_score = -1000000000.0
wide_limits = (1, 2, 3, 4, 5, 6, 7, 8, 12, 16, 23, 32, 46, 64, 91)
causal_limits = tuple(range(1, 16)) + (
    16, 19, 21, 24, 27, 31, 35, 40, 46, 52, 59, 67, 77, 87, 99, 113,
)


def nn(a, b):
    return lax.dot_general(a, b, (((1,), (0,)), ((), ())), preferred_element_type=F32)


def nt(a, b):
    return lax.dot_general(a, b, (((1,), (1,)), ((), ())), preferred_element_type=F32)


def tn(a, b):
    return lax.dot_general(a, b, (((0,), (0,)), ((), ())), preferred_element_type=F32)


def iota(shape, axis):
    return lax.broadcasted_iota(jnp.int32, shape, axis)


def rms(v, gain):
    return v * lax.rsqrt(jnp.mean(v * v, axis=-1, keepdims=True) + norm_epsilon) * gain


def rms_back(v, gain, e):
    s = lax.rsqrt(jnp.mean(v * v, axis=-1, keepdims=True) + norm_epsilon)
    eg = e * gain
    vs = v * s
    grad = s * (eg - vs * (s * jnp.mean(eg * v, axis=-1, keepdims=True)))
    return grad, jnp.sum(e * vs, axis=0, keepdims=True)


def gelu_cdf(x):
    return 0.5 * (1.0 + lax.erf(x * 0.7071067811865476))


def gelu_slope(x, cdf):
    return cdf + x * (0.3989422804014327 * jnp.exp(-0.5 * x * x))


class Refs:
    pass


class Group:
    def __init__(self, r, rows):
        self.r = r
        self.rows = rows
        self.t = lax.axis_index("tok")
        self.f = lax.axis_index("ffn")
        self.c = self.f % 2
        self.sib = self.f + 1 - 2 * self.c
        self.cross = (self.f + 2) % GROUP
        self.diag = (self.sib + 2) % GROUP
        self.near = (self.f // 2) * (2 * rows)
        self.far = 2 * rows - self.near
        self.count = 0

    def slot(self, index):
        return pl.ds(pl.multiple_of(index * self.rows, 16), self.rows)

    def near_rows(self):
        return pl.ds(pl.multiple_of(self.near, 16), 2 * self.rows)

    def far_rows(self):
        return pl.ds(pl.multiple_of(self.far, 16), 2 * self.rows)

    def signal(self):
        barrier = pltpu.get_barrier_semaphore()
        for other in (self.sib, self.cross, self.diag):
            pl.semaphore_signal(barrier, inc=1, device_id=(self.t, other), device_id_type=MESH)

    def wait(self):
        pl.semaphore_wait(pltpu.get_barrier_semaphore(), 3)

    def copy(self, src, dst, other):
        k = self.count
        self.count += 1
        return pltpu.make_async_remote_copy(
            src_ref=src,
            dst_ref=dst,
            send_sem=self.r.send.at[k],
            recv_sem=self.r.recv.at[k],
            device_id=(self.t, other),
            device_id_type=MESH,
        )


class Gather:
    def __init__(self, g, ref):
        self.g, self.ref = g, ref
        own = ref.at[g.slot(g.f), :]
        self.x = g.copy(own, own, g.cross)
        self.s = g.copy(own, own, g.sib)
        got = ref.at[g.slot(g.cross), :]
        self.h = g.copy(got, got, g.sib)

    def start(self):
        self.x.start()
        self.s.start()

    def near(self):
        self.s.wait_recv()

    def relay(self):
        self.x.wait_recv()
        self.h.start()

    def far(self):
        self.h.wait_recv()

    def done(self):
        self.x.wait_send()
        self.s.wait_send()
        self.h.wait_send()


class Scatter:
    def __init__(self, g, near_f32, far_low, sib_low, sum_low, got):
        self.g = g
        self.near_f32, self.far_low, self.sib_low, self.sum_low, self.got = (
            near_f32, far_low, sib_low, sum_low, got,
        )
        self.a = g.copy(far_low.at[1 - g.c], got.at[0], g.sib)
        self.b = g.copy(sib_low, got.at[1], g.sib)
        self.x = g.copy(sum_low, got.at[2], g.cross)

    def put_far(self, value):
        rows = self.g.rows
        low = value.astype(BF)
        self.far_low[0] = low[:rows]
        self.far_low[1] = low[rows:]
        self.a.start()

    def put_near(self, value):
        rows = self.g.rows
        self.near_f32[0] = value[:rows]
        self.near_f32[1] = value[rows:]
        self.sib_low[...] = self.near_f32[1 - self.g.c].astype(BF)
        self.b.start()

    def relay(self):
        self.a.wait_recv()
        total = self.got[0].astype(F32) + self.far_low[self.g.c].astype(F32)
        self.sum_low[...] = total.astype(BF)
        self.x.start()

    def result(self):
        self.b.wait_recv()
        part = self.near_f32[self.g.c] + self.got[1].astype(F32)
        self.x.wait_recv()
        return part + self.got[2].astype(F32)

    def done(self):
        self.a.wait_send()
        self.b.wait_send()
        self.x.wait_send()


def scatter_scratch(tag, rows, width):
    return {
        tag + "_near": ((2, rows, width), F32),
        tag + "_far": ((2, rows, width), BF),
        tag + "_sib": ((rows, width), BF),
        tag + "_sum": ((rows, width), BF),
        tag + "_got": ((3, rows, width), BF),
    }


def scatter_of(g, r, tag):
    return Scatter(
        g,
        getattr(r, tag + "_near"),
        getattr(r, tag + "_far"),
        getattr(r, tag + "_sib"),
        getattr(r, tag + "_sum"),
        getattr(r, tag + "_got"),
    )


class Exchange:
    def __init__(self, g, src, dst):
        self.g, self.src, self.dst = g, src, dst
        self.copies = [
            g.copy(src.at[g.slot(other), :], dst.at[g.f], other)
            for other in (g.diag, g.cross, g.sib)
        ]

    def start(self):
        for copy in self.copies:
            copy.start()
        self.dst[self.g.f] = self.src[self.g.slot(self.g.f), :]

    def recv(self):
        for copy in self.copies:
            copy.wait_recv()

    def done(self):
        for copy in self.copies:
            copy.wait_send()


def merged_out(dst, w_out):
    width = dst.shape[2]
    total = nn(dst[0], w_out[:width, :])
    for p in range(1, GROUP):
        total = total + nn(dst[p], w_out[p * width : (p + 1) * width, :])
    return total


def run(name, cid, body, ins, outs, scratch, copies, rows):
    in_names, out_names, scr_names = list(ins), list(outs), list(scratch)

    def kernel(*refs):
        r = Refs()
        for n, ref in zip(in_names + out_names + scr_names + ["send", "recv"], refs):
            setattr(r, n, ref)
        body(r, Group(r, rows))

    spaces = {"v": pltpu.VMEM, "s": pltpu.SMEM}
    got = pl.pallas_call(
        kernel,
        out_shape=[jax.ShapeDtypeStruct(*outs[n]) for n in out_names],
        in_specs=[pl.BlockSpec(memory_space=spaces[ins[n][1]]) for n in in_names],
        out_specs=[pl.BlockSpec(memory_space=pltpu.VMEM) for n in out_names],
        scratch_shapes=[pltpu.VMEM(*scratch[n]) for n in scr_names]
        + [pltpu.SemaphoreType.DMA((copies,)), pltpu.SemaphoreType.DMA((copies,))],
        compiler_params=pltpu.CompilerParams(
            collective_id=cid, has_side_effects=True, vmem_limit_bytes=62 * 2**20
        ),
        name=name,
    )(*[ins[n][0] for n in in_names])
    return dict(zip(out_names, got))


def enc_starts(lens, count):
    starts = [jnp.int32(0)]
    for e in range(count):
        starts.append(starts[-1] + lens[0, e])
    return starts


def segment_of(place, starts):
    total = jnp.zeros(place.shape, jnp.int32)
    for s in starts[1:-1]:
        total = total + (place >= s).astype(jnp.int32)
    return total


def enc_bias_blocks(tables, out, f, heads, blocks):
    side = SLOT
    r = iota((side, side), 1) - iota((side, side), 0)
    for d in range(-(blocks - 1), blocks):
        far = blocks - 1 + d
        if abs(d) >= 2:
            for h in range(heads):
                value = tables[0, 31 if d > 0 else 15, f * heads + h]
                out[h, far] = jnp.full((side, side), value, F32)
            continue
        rel = r + d * side
        values = [jnp.full((side, side), tables[0, 0 if d <= 0 else 17, f * heads + h], F32) for h in range(heads)]
        if d >= 0:
            for b, limit in enumerate(wide_limits):
                hit = rel >= limit
                values = [
                    jnp.where(hit, tables[0, 17 + b, f * heads + h], values[h]) for h in range(heads)
                ]
        if d <= 0:
            for b, limit in enumerate(wide_limits):
                hit = rel <= -limit
                values = [
                    jnp.where(hit, tables[0, 1 + b, f * heads + h], values[h]) for h in range(heads)
                ]
        for h in range(heads):
            out[h, far] = values[h]


def dec_bias_block(tables, out, f, heads):
    side = SLOT
    m = iota((side, side), 0) - iota((side, side), 1)
    values = [jnp.full((side, side), tables[1, 0, f * heads + h], F32) for h in range(heads)]
    for b, limit in enumerate(causal_limits):
        hit = m >= limit
        values = [jnp.where(hit, tables[1, 1 + b, f * heads + h], values[h]) for h in range(heads)]
    for h in range(heads):
        out[h] = values[h]


def put_heads(ref, rows, value, first):
    low = value.astype(BF)
    for j in range(low.shape[1] // DH):
        ref[first + j, rows, :] = low[:, j * DH : (j + 1) * DH]


def softmax_low(scores):
    top = jnp.max(scores, axis=-1, keepdims=True)
    raised = jnp.exp(scores - top)
    return (raised * (1.0 / jnp.sum(raised, axis=-1, keepdims=True))).astype(BF)


def enc_attend(qkv, probs, mixed, bias, starts, heads, packed):
    blocks = packed // SLOT
    seg_keys = segment_of(iota((1, packed), 1), starts)

    @pl.loop(0, blocks)
    def _(i):
        rows = pl.ds(pl.multiple_of(i * SLOT, SLOT), SLOT)
        seg_rows = segment_of(iota((SLOT, 1), 0) + i * SLOT, starts)
        live = seg_rows == seg_keys
        for h in range(heads):
            scores = nt(qkv[h, rows, :], qkv[heads + h])
            add = jnp.concatenate([bias[h, j - i + blocks - 1] for j in range(blocks)], axis=1)
            low = softmax_low(jnp.where(live, scores + add, masked_score))
            probs[h, rows, :] = low
            mixed[rows, h * DH : (h + 1) * DH] = nn(low, qkv[2 * heads + h]).astype(BF)


def cross_attend(qkv, probs, mixed, lens, heads, packed):
    blocks = packed // SLOT
    starts = enc_starts(lens, blocks)
    place = iota((1, packed), 1)
    seg_keys = segment_of(place, starts)

    @pl.loop(0, blocks)
    def _(i):
        rows = pl.ds(pl.multiple_of(i * SLOT, SLOT), SLOT)
        live = seg_keys == i
        for h in range(heads):
            scores = nt(qkv[h, rows, :], qkv[heads + h])
            low = softmax_low(jnp.where(live, scores, masked_score))
            probs[h, rows, :] = low
            mixed[rows, h * DH : (h + 1) * DH] = nn(low, qkv[2 * heads + h]).astype(BF)


def self_attend(qkv, probs, mixed, bias, lens, heads, packed):
    place = iota((SLOT, SLOT), 1)
    lower = place <= iota((SLOT, SLOT), 0)

    @pl.loop(0, packed // SLOT)
    def _(i):
        rows = pl.ds(pl.multiple_of(i * SLOT, SLOT), SLOT)
        live = lower & (place < lens[0, i])
        for h in range(heads):
            scores = nt(qkv[h, rows, :], qkv[heads + h, rows, :])
            low = softmax_low(jnp.where(live, scores + bias[h], masked_score))
            probs[h, rows, :] = low
            mixed[rows, h * DH : (h + 1) * DH] = nn(low, qkv[2 * heads + h, rows, :]).astype(BF)


def score_grads(low, grad_mix, values):
    weights = low.astype(F32)
    part = weights * nt(grad_mix, values)
    return (part - weights * jnp.sum(part, axis=-1, keepdims=True)).astype(BF)


def full_attend_back(qkv, probs, grad_mixed, ds, grads, heads, packed):
    width = heads * DH

    @pl.loop(0, packed // SLOT)
    def _(i):
        rows = pl.ds(pl.multiple_of(i * SLOT, SLOT), SLOT)
        for h in range(heads):
            cols = slice(h * DH, (h + 1) * DH)
            low = score_grads(probs[h, rows, :], grad_mixed[rows, cols], qkv[2 * heads + h])
            ds[h, rows, :] = low
            grads[rows, cols] = nn(low, qkv[heads + h]).astype(BF)

    for h in range(heads):
        cols = slice(h * DH, (h + 1) * DH)
        grads[:, width + h * DH : width + (h + 1) * DH] = tn(ds[h], qkv[h]).astype(BF)
        grads[:, 2 * width + h * DH : 2 * width + (h + 1) * DH] = tn(
            probs[h], grad_mixed[:, cols]
        ).astype(BF)


def self_attend_back(qkv, probs, grad_mixed, ds_sum, grads, heads, packed):
    width = heads * DH
    for h in range(heads):
        ds_sum[h] = jnp.zeros((SLOT, SLOT), F32)

    @pl.loop(0, packed // SLOT)
    def _(i):
        rows = pl.ds(pl.multiple_of(i * SLOT, SLOT), SLOT)
        for h in range(heads):
            cols = slice(h * DH, (h + 1) * DH)
            prob = probs[h, rows, :]
            gm = grad_mixed[rows, cols]
            low = score_grads(prob, gm, qkv[2 * heads + h, rows, :])
            ds_sum[h] = ds_sum[h] + low.astype(F32)
            grads[rows, cols] = nn(low, qkv[heads + h, rows, :]).astype(BF)
            grads[rows, width + h * DH : width + (h + 1) * DH] = tn(low, qkv[h, rows, :]).astype(BF)
            grads[rows, 2 * width + h * DH : 2 * width + (h + 1) * DH] = tn(prob, gm).astype(BF)


def bucket_sums(pieces):
    return [jnp.sum(p, axis=1, keepdims=True) for p in pieces]


def put_table(out, lines, f, heads):
    lane = iota((BUCKETS, 128), 1)
    total = jnp.zeros((BUCKETS, 128), F32)
    for h in range(heads):
        summed = jnp.sum(lines[h], axis=1, keepdims=True)
        total = jnp.where(lane == f * heads + h, summed, total)
    out[...] = total


def dec_table_grad(ds_sum, line, out, f, heads):
    m = iota((SLOT, SLOT), 0) - iota((SLOT, SLOT), 1)
    limits = (0,) + causal_limits + (SLOT,)
    for b in range(BUCKETS):
        hit = (m >= limits[b]) & (m < limits[b + 1]) if b else m <= 0
        for h in range(heads):
            line[h, b : b + 1, :] = jnp.sum(
                jnp.where(hit, ds_sum[h], 0.0), axis=0, keepdims=True
            )
    put_table(out, [line[h] for h in range(heads)], f, heads)


def enc_table_grad(ds, ds_sum, line, out, f, heads, packed):
    blocks = packed // SLOT
    zero = jnp.zeros((SLOT, SLOT), F32)
    r = iota((SLOT, SLOT), 1) - iota((SLOT, SLOT), 0)
    limits = wide_limits + (10**6,)
    for h in range(heads):
        for slot in range(5):
            total = zero
            for i in range(blocks):
                for j in range(blocks):
                    if max(-2, min(2, j - i)) == slot - 2:
                        total = total + ds[h, i * SLOT : (i + 1) * SLOT, j * SLOT : (j + 1) * SLOT].astype(F32)
            ds_sum[h, slot] = total
    for h in range(heads):
        line[h] = jnp.zeros((BUCKETS, SLOT), F32)
        line[h, 0:1, :] = jnp.sum(jnp.where(r == 0, ds_sum[h, 2], 0.0), axis=0, keepdims=True)
    for b in range(15):
        low, high = limits[b], limits[b + 1]
        for side in (1, -1):
            rel = side * r
            hit_same = (rel >= low) & (rel < high)
            hit_next = (rel + SLOT >= low) & (rel + SLOT < high)
            row = 1 + b + (16 if side > 0 else 0)
            for h in range(heads):
                total = jnp.where(hit_same, ds_sum[h, 2], 0.0) + jnp.where(
                    hit_next, ds_sum[h, 2 + side], 0.0
                )
                if b == 14:
                    total = total + ds_sum[h, 2 + 2 * side]
                line[h, row : row + 1, :] = jnp.sum(total, axis=0, keepdims=True)
    put_table(out, [line[h] for h in range(heads)], f, heads)


def kernel_a(r, g):
    rows, f = g.rows, g.f
    packed = GROUP * rows
    heads = r.qkv_e.shape[0] // 3
    g.signal()
    own = g.slot(f)
    r.gath_a[own, :] = rms(r.enc_in[...].astype(F32), r.gains[0:1, :]).astype(BF)
    r.gath_c[own, :] = rms(r.dec_in[...].astype(F32), r.gains[3:4, :]).astype(BF)
    r.gath_g[own, :] = r.cot[...]
    ga, gc, gg = Gather(g, r.gath_a), Gather(g, r.gath_c), Gather(g, r.gath_g)
    xe, xd = Exchange(g, r.mixed_e, r.merged_e), Exchange(g, r.mixed_d, r.merged_d)
    g.wait()
    ga.start()
    gc.start()
    gg.start()
    enc_bias_blocks(r.tables, r.bias_e, f, heads, packed // SLOT)
    dec_bias_block(r.tables, r.bias_d, f, heads)
    ga.relay()
    ga.near()
    near, far = g.near_rows(), g.far_rows()
    put_heads(r.qkv_e, near, nn(r.gath_a[near, :], r.w_e[...]), 0)
    ga.far()
    put_heads(r.qkv_e, far, nn(r.gath_a[far, :], r.w_e[...]), 0)
    gc.relay()
    enc_attend(
        r.qkv_e, r.probs_e, r.mixed_e, r.bias_e, enc_starts(r.enc_lens, packed // SLOT), heads, packed
    )
    xe.start()
    gc.near()
    put_heads(r.qkv_d, near, nn(r.gath_c[near, :], r.w_d[...]), 0)
    gc.far()
    put_heads(r.qkv_d, far, nn(r.gath_c[far, :], r.w_d[...]), 0)
    self_attend(r.qkv_d, r.probs_d, r.mixed_d, r.bias_d, r.dec_lens, heads, packed)
    xd.start()
    gg.relay()
    xe.recv()
    r.x1[...] = r.enc_in[...].astype(F32) + merged_out(r.merged_e, r.wo_e)
    xd.recv()
    r.d1[...] = r.dec_in[...].astype(F32) + merged_out(r.merged_d, r.wo_d)
    gg.near()
    gg.far()
    for item in (ga, gc, gg, xe, xd):
        item.done()


def kernel_b(r, g):
    rows, f = g.rows, g.f
    packed = GROUP * rows
    heads = r.qkv_c.shape[0] // 3
    g.signal()
    own = g.slot(f)
    r.gath_b[own, :] = rms(r.x1[...], r.gains[1:2, :]).astype(BF)
    r.gath_d[own, :] = rms(r.d1[...], r.gains[4:5, :]).astype(BF)
    gb, gd, gm = Gather(g, r.gath_b), Gather(g, r.gath_d), Gather(g, r.gath_m)
    rs = scatter_of(g, r, "rs")
    xc = Exchange(g, r.mixed_c, r.merged_c)
    near, far = g.near_rows(), g.far_rows()
    g.wait()
    gb.start()
    gd.start()

    def hidden_of(part):
        pre = nn(r.gath_b[part, :], r.w_in[...])
        r.pre[part, :] = pre
        r.hidden[part, :] = (pre * gelu_cdf(pre)).astype(BF)

    gb.near()
    hidden_of(near)
    gb.relay()
    gb.far()
    hidden_of(far)
    rs.put_far(nn(r.hidden[far, :], r.w_down[...]))
    rs.put_near(nn(r.hidden[near, :], r.w_down[...]))
    rs.relay()
    gd.relay()
    gd.near()
    put_heads(r.qkv_c, near, nn(r.gath_d[near, :], r.w_q[...]), 0)
    gd.far()
    put_heads(r.qkv_c, far, nn(r.gath_d[far, :], r.w_q[...]), 0)
    x2 = r.x1[...] + rs.result()
    r.x2[...] = x2
    r.gath_m[own, :] = rms(x2, r.gains[2:3, :]).astype(BF)
    gm.start()
    gm.near()
    put_heads(r.qkv_c, near, nn(r.gath_m[near, :], r.w_kv[...]), heads)
    gm.relay()
    gm.far()
    put_heads(r.qkv_c, far, nn(r.gath_m[far, :], r.w_kv[...]), heads)
    cross_attend(r.qkv_c, r.probs_c, r.mixed_c, r.enc_lens, heads, packed)
    xc.start()
    xc.recv()
    r.d2[...] = r.d1[...] + merged_out(r.merged_c, r.wo_c)
    for item in (gb, gd, gm, rs, xc):
        item.done()


def kernel_c(r, g):
    rows, f = g.rows, g.f
    g.signal()
    own = g.slot(f)
    r.gath_e[own, :] = rms(r.d2[...], r.gains[5:6, :]).astype(BF)
    ge = Gather(g, r.gath_e)
    rb, rf = scatter_of(g, r, "rb"), scatter_of(g, r, "rf")
    near, far = g.near_rows(), g.far_rows()
    g.wait()
    ge.start()

    def backward_of(part):
        pre = nn(r.gath_e[part, :], r.w_in[...])
        cdf = gelu_cdf(pre)
        r.hidden[part, :] = (pre * cdf).astype(BF)
        back = r.grad_hidden[part, :].astype(F32) * gelu_slope(pre, cdf)
        r.grad_pre[part, :] = back.astype(BF)

    r.grad_hidden[near, :] = nt(r.gath_g[near, :], r.w_down[...]).astype(BF)
    r.grad_hidden[far, :] = nt(r.gath_g[far, :], r.w_down[...]).astype(BF)
    ge.near()
    backward_of(near)
    ge.relay()
    ge.far()
    backward_of(far)
    rb.put_far(nt(r.grad_pre[far, :], r.w_in[...]))
    rb.put_near(nt(r.grad_pre[near, :], r.w_in[...]))
    rb.relay()
    rf.put_far(nn(r.hidden[far, :], r.w_down[...]))
    rf.put_near(nn(r.hidden[near, :], r.w_down[...]))
    rf.relay()
    r.unit_in[...] = tn(r.gath_e[...], r.grad_pre[...]).astype(BF)
    r.unit_down[...] = tn(r.gath_g[...], r.hidden[...]).astype(BF)
    d2 = r.d2[...]
    grad, gain = rms_back(d2, r.gains[5:6, :], rb.result())
    r.g2[...] = r.cot[...].astype(F32) + grad
    r.gain[...] = gain
    r.dec_out[...] = (d2 + rf.result()).astype(BF)
    for item in (ge, rb, rf):
        item.done()


def kernel_d(r, g):
    rows, f = g.rows, g.f
    packed = GROUP * rows
    heads = r.qkv_c.shape[0] // 3
    width = heads * DH
    g.signal()
    own = g.slot(f)
    r.gath_g2[own, :] = r.g2[...].astype(BF)
    gg = Gather(g, r.gath_g2)
    rm, rq = scatter_of(g, r, "rm"), scatter_of(g, r, "rq")
    near, far = g.near_rows(), g.far_rows()
    g.wait()
    gg.start()
    gg.near()
    r.grad_mixed[near, :] = nt(r.gath_g2[near, :], r.wo_part[...]).astype(BF)
    gg.relay()
    gg.far()
    r.grad_mixed[far, :] = nt(r.gath_g2[far, :], r.wo_part[...]).astype(BF)
    full_attend_back(r.qkv_c, r.probs_c, r.grad_mixed, r.ds, r.grads, heads, packed)
    rm.put_far(nt(r.grads[far, width:], r.w_kv[...]))
    rm.put_near(nt(r.grads[near, width:], r.w_kv[...]))
    rm.relay()
    rq.put_far(nt(r.grads[far, :width], r.w_q[...]))
    rq.put_near(nt(r.grads[near, :width], r.w_q[...]))
    rq.relay()
    r.unit[:, :width] = tn(r.gath_d[...], r.grads[:, :width]).astype(BF)
    r.unit[:, width : 3 * width] = tn(r.gath_m[...], r.grads[:, width:]).astype(BF)
    r.unit[:, 3 * width :] = tn(r.gath_g2[...], r.mixed_c[...]).astype(BF)
    grad, gain = rms_back(r.x2[...], r.gains[2:3, :], rm.result())
    r.g_last[...] = grad
    r.gain_m[...] = gain
    grad, gain = rms_back(r.d1[...], r.gains[4:5, :], rq.result())
    r.g1[...] = r.g2[...] + grad
    r.gain_d[...] = gain
    for item in (gg, rm, rq):
        item.done()


def kernel_e(r, g):
    rows, f = g.rows, g.f
    packed = GROUP * rows
    heads = r.qkv_d.shape[0] // 3
    width = heads * DH
    g.signal()
    own = g.slot(f)
    r.gath_l[own, :] = r.g_last[...].astype(BF)
    r.gath_g1[own, :] = r.g1[...].astype(BF)
    gl, gg = Gather(g, r.gath_l), Gather(g, r.gath_g1)
    rf, rd = scatter_of(g, r, "rf"), scatter_of(g, r, "rd")
    near, far = g.near_rows(), g.far_rows()
    g.wait()
    gl.start()
    gg.start()

    def backward_of(part):
        pre = r.pre[part, :]
        back = nt(r.gath_l[part, :], r.w_down[...]).astype(BF).astype(F32) * gelu_slope(pre, gelu_cdf(pre))
        r.grad_pre[part, :] = back.astype(BF)

    gl.near()
    backward_of(near)
    gl.relay()
    gl.far()
    backward_of(far)
    rf.put_far(nt(r.grad_pre[far, :], r.w_in[...]))
    rf.put_near(nt(r.grad_pre[near, :], r.w_in[...]))
    rf.relay()
    gg.relay()
    gg.near()
    r.grad_mixed[near, :] = nt(r.gath_g1[near, :], r.wo_part[...]).astype(BF)
    gg.far()
    r.grad_mixed[far, :] = nt(r.gath_g1[far, :], r.wo_part[...]).astype(BF)
    self_attend_back(r.qkv_d, r.probs_d, r.grad_mixed, r.ds_sum, r.grads, heads, packed)
    rd.put_far(nt(r.grads[far, :], r.w_d[...]))
    rd.put_near(nt(r.grads[near, :], r.w_d[...]))
    rd.relay()
    grad, gain = rms_back(r.x1[...], r.gains[1:2, :], rf.result())
    r.g_mid[...] = r.g_last[...] + grad
    r.gain_b[...] = gain
    r.unit_in[...] = tn(r.gath_b[...], r.grad_pre[...]).astype(BF)
    r.unit_down[...] = tn(r.gath_l[...], r.hidden[...]).astype(BF)
    r.unit[:, : 3 * width] = tn(r.gath_c[...], r.grads[...]).astype(BF)
    r.unit[:, 3 * width :] = tn(r.gath_g1[...], r.mixed_d[...]).astype(BF)
    dec_table_grad(r.ds_sum, r.line, r.table, f, heads)
    grad, gain = rms_back(r.dec_in[...].astype(F32), r.gains[3:4, :], rd.result())
    r.dec_grad[...] = (r.g1[...] + grad).astype(BF)
    r.gain_c[...] = gain
    for item in (gl, gg, rf, rd):
        item.done()


def kernel_f(r, g):
    rows, f = g.rows, g.f
    packed = GROUP * rows
    heads = r.qkv_e.shape[0] // 3
    width = heads * DH
    g.signal()
    own = g.slot(f)
    r.gath_gm[own, :] = r.g_mid[...].astype(BF)
    gg = Gather(g, r.gath_gm)
    rs = scatter_of(g, r, "rs")
    near, far = g.near_rows(), g.far_rows()
    g.wait()
    gg.start()
    gg.near()
    r.grad_mixed[near, :] = nt(r.gath_gm[near, :], r.wo_part[...]).astype(BF)
    gg.relay()
    gg.far()
    r.grad_mixed[far, :] = nt(r.gath_gm[far, :], r.wo_part[...]).astype(BF)
    full_attend_back(r.qkv_e, r.probs_e, r.grad_mixed, r.ds, r.grads, heads, packed)
    rs.put_far(nt(r.grads[far, :], r.w_e[...]))
    rs.put_near(nt(r.grads[near, :], r.w_e[...]))
    rs.relay()
    r.unit[:, : 3 * width] = tn(r.gath_a[...], r.grads[...]).astype(BF)
    r.unit[:, 3 * width :] = tn(r.gath_gm[...], r.mixed_e[...]).astype(BF)
    enc_table_grad(r.ds, r.ds_sum, r.line, r.table, f, heads, packed)
    grad, gain = rms_back(r.enc_in[...].astype(F32), r.gains[0:1, :], rs.result())
    r.enc_grad[...] = (r.g_mid[...] + grad).astype(BF)
    r.gain[...] = gain
    for item in (gg, rs):
        item.done()


def on_device(
    enc_in,
    dec_in,
    cotangent,
    enc_lengths,
    dec_lengths,
    qk_weights,
    v_weights,
    out_weights,
    ffn_in,
    ffn_out,
    bias_tables,
    gains,
):
    group_size = lax.axis_size("ffn")
    f = lax.axis_index("ffn")
    rows, model = enc_in.shape
    packed = rows * group_size
    width = qk_weights.shape[3] // group_size
    heads = width // DH
    hidden = ffn_in.shape[2]
    side = SLOT

    def cut(weights, axis):
        return lax.dynamic_slice_in_dim(weights, f * width, width, axis)

    qk_cut, v_cut = cut(qk_weights, 3), cut(v_weights, 2)
    w_qkv = [jnp.concatenate([qk_cut[l, 0], qk_cut[l, 1], v_cut[l]], axis=1) for l in range(2)]
    w_q, w_kv = qk_cut[2, 0], jnp.concatenate([qk_cut[2, 1], v_cut[2]], axis=1)
    wo_part = cut(out_weights, 1)

    low = lambda *shape: (shape, BF)
    wide = lambda *shape: (shape, F32)
    v = lambda a: (a, "v")
    s = lambda a: (a, "s")
    call = functools.partial(run, rows=rows)

    a = call(
        "self_attentions", 1, kernel_a,
        dict(
            enc_in=v(enc_in), dec_in=v(dec_in), cot=v(cotangent), gains=v(gains), tables=s(bias_tables),
            enc_lens=s(enc_lengths), dec_lens=s(dec_lengths), w_e=v(w_qkv[0]), w_d=v(w_qkv[1]),
            wo_e=v(out_weights[0]), wo_d=v(out_weights[1]),
        ),
        dict(
            gath_a=low(packed, model), gath_c=low(packed, model), gath_g=low(packed, model),
            qkv_e=low(3 * heads, packed, DH), qkv_d=low(3 * heads, packed, DH),
            probs_e=low(heads, packed, packed), probs_d=low(heads, packed, side),
            mixed_e=low(packed, width), mixed_d=low(packed, width),
            x1=wide(rows, model), d1=wide(rows, model),
        ),
        dict(
            bias_e=wide(heads, 2 * (packed // side) - 1, side, side), bias_d=wide(heads, side, side),
            merged_e=low(GROUP, rows, width), merged_d=low(GROUP, rows, width),
        ),
        15,
    )
    b = call(
        "encoder_ffn_cross", 2, kernel_b,
        dict(
            x1=v(a["x1"]), d1=v(a["d1"]), gains=v(gains), enc_lens=s(enc_lengths),
            w_in=v(ffn_in[0]), w_down=v(ffn_out[0]), w_q=v(w_q), w_kv=v(w_kv), wo_c=v(out_weights[2]),
        ),
        dict(
            gath_b=low(packed, model), gath_d=low(packed, model), gath_m=low(packed, model),
            pre=wide(packed, hidden), hidden=low(packed, hidden),
            qkv_c=low(3 * heads, packed, DH), probs_c=low(heads, packed, packed),
            mixed_c=low(packed, width), x2=wide(rows, model), d2=wide(rows, model),
        ),
        dict(merged_c=low(GROUP, rows, width), **scatter_scratch("rs", rows, model)),
        15,
    )
    c = call(
        "decoder_ffn", 3, kernel_c,
        dict(
            d2=v(b["d2"]), cot=v(cotangent), gath_g=v(a["gath_g"]), gains=v(gains),
            w_in=v(ffn_in[1]), w_down=v(ffn_out[1]),
        ),
        dict(
            dec_out=low(rows, model), g2=wide(rows, model), gain=wide(1, model),
            unit_in=low(model, hidden), unit_down=low(model, hidden),
        ),
        dict(
            gath_e=low(packed, model), hidden=low(packed, hidden), grad_hidden=low(packed, hidden),
            grad_pre=low(packed, hidden),
            **scatter_scratch("rb", rows, model), **scatter_scratch("rf", rows, model),
        ),
        9,
    )
    d = call(
        "cross_back", 4, kernel_d,
        dict(
            g2=v(c["g2"]), x2=v(b["x2"]), d1=v(a["d1"]), gains=v(gains), gath_d=v(b["gath_d"]),
            gath_m=v(b["gath_m"]), qkv_c=v(b["qkv_c"]), probs_c=v(b["probs_c"]), mixed_c=v(b["mixed_c"]),
            w_q=v(w_q), w_kv=v(w_kv), wo_part=v(wo_part[2]),
        ),
        dict(
            g_last=wide(rows, model), g1=wide(rows, model), unit=low(model, 4 * width),
            gain_m=wide(1, model), gain_d=wide(1, model),
        ),
        dict(
            gath_g2=low(packed, model), grad_mixed=low(packed, width), ds=low(heads, packed, packed),
            grads=low(packed, 3 * width),
            **scatter_scratch("rm", rows, model), **scatter_scratch("rq", rows, model),
        ),
        9,
    )
    e = call(
        "encoder_ffn_self_back", 5, kernel_e,
        dict(
            g_last=v(d["g_last"]), g1=v(d["g1"]), x1=v(a["x1"]), dec_in=v(dec_in), gains=v(gains),
            gath_b=v(b["gath_b"]), gath_c=v(a["gath_c"]), pre=v(b["pre"]), hidden=v(b["hidden"]),
            w_in=v(ffn_in[0]), w_down=v(ffn_out[0]), qkv_d=v(a["qkv_d"]), probs_d=v(a["probs_d"]),
            mixed_d=v(a["mixed_d"]), w_d=v(w_qkv[1]), wo_part=v(wo_part[1]),
        ),
        dict(
            g_mid=wide(rows, model), dec_grad=low(rows, model), unit_in=low(model, hidden),
            unit_down=low(model, hidden), unit=low(model, 4 * width), gain_b=wide(1, model),
            gain_c=wide(1, model), table=wide(BUCKETS, 128),
        ),
        dict(
            gath_l=low(packed, model), gath_g1=low(packed, model), grad_pre=low(packed, hidden),
            grad_mixed=low(packed, width), grads=low(packed, 3 * width), ds_sum=wide(heads, side, side),
            line=wide(heads, BUCKETS, side),
            **scatter_scratch("rf", rows, model), **scatter_scratch("rd", rows, model),
        ),
        12,
    )
    h = call(
        "encoder_self_back", 6, kernel_f,
        dict(
            g_mid=v(e["g_mid"]), enc_in=v(enc_in), gains=v(gains), gath_a=v(a["gath_a"]),
            qkv_e=v(a["qkv_e"]), probs_e=v(a["probs_e"]), mixed_e=v(a["mixed_e"]), w_e=v(w_qkv[0]),
            wo_part=v(wo_part[0]),
        ),
        dict(
            enc_grad=low(rows, model), unit=low(model, 4 * width), gain=wide(1, model),
            table=wide(BUCKETS, 128),
        ),
        dict(
            gath_gm=low(packed, model), grad_mixed=low(packed, width), ds=low(heads, packed, packed),
            grads=low(packed, 3 * width), ds_sum=wide(heads, 5, side, side), line=wide(heads, BUCKETS, side),
            **scatter_scratch("rs", rows, model),
        ),
        6,
    )

    def summed(units):
        return lax.psum_scatter(jnp.stack(units), "tok", scatter_dimension=1, tiled=True)

    early = summed([c["unit_in"], c["unit_down"], d["unit"]]).astype(F32)
    late = summed([e["unit"], e["unit_in"], e["unit_down"], h["unit"]]).astype(F32)
    dec_up, dec_down, cross = early[0], early[1], early[2]
    self_unit, enc_up, enc_down, enc_unit = late[0], late[1], late[2], late[3]
    layers = (enc_unit, self_unit, cross)
    qk_grad = jnp.stack([jnp.stack([u[:, :width], u[:, width : 2 * width]]) for u in layers])
    v_grad = jnp.stack([u[:, 2 * width : 3 * width] for u in layers])
    out_grad = jnp.stack([u[:, 3 * width :].T for u in layers])
    up_grad = jnp.stack([enc_up, dec_up])
    down_grad = jnp.stack([enc_down.T, dec_down.T])
    gain_terms = jnp.concatenate(
        [h["gain"], e["gain_b"], d["gain_m"], e["gain_c"], d["gain_d"], c["gain"]], axis=0
    )
    table_terms = jnp.stack([h["table"], e["table"]])
    gain_grad, table_grad = lax.psum((gain_terms, table_terms), ("tok", "ffn"))
    return (
        c["dec_out"],
        h["enc_grad"],
        e["dec_grad"],
        qk_grad,
        v_grad,
        out_grad,
        up_grad,
        down_grad,
        table_grad[:, :, : bias_tables.shape[2]],
        gain_grad,
        gain_grad[5],
    )


def solution(mesh):
    placed = (
        P(("tok", "ffn"), None),
        P(("tok", "ffn"), None),
        P(("tok", "ffn"), None),
        P("tok", None),
        P("tok", None),
        P(),
        P(),
        P(),
        P(None, None, "ffn"),
        P(None, "ffn", None),
        P(),
        P(),
    )
    return jax.shard_map(
        on_device,
        mesh=mesh,
        in_specs=placed,
        out_specs=(
            P(("tok", "ffn"), None),
            P(("tok", "ffn"), None),
            P(("tok", "ffn"), None),
            P(None, None, "tok", "ffn"),
            P(None, "tok", "ffn"),
            P(None, "ffn", "tok"),
            P(None, "tok", "ffn"),
            P(None, "ffn", "tok"),
            P(),
            P(),
            P(),
        ),
        check_vma=False,
    )
```

```python
import functools
import jax
import jax.numpy as jnp
from jax import lax
from jax.experimental import pallas as pl
from jax.experimental.pallas import tpu as pltpu
from jax.sharding import PartitionSpec as P

DH = 64
BUCKETS = 32
SLOT = 128
GROUP = 4
VMEM_LIMIT = 64 * 2**20 - 2**18
BF = jnp.bfloat16
F32 = jnp.float32
MESH = pl.DeviceIdType.MESH

norm_epsilon = 1e-06
masked_score = -1000000000.0
wide_limits = (1, 2, 3, 4, 5, 6, 7, 8, 12, 16, 23, 32, 46, 64, 91)
causal_limits = tuple(range(1, 16)) + (
    16, 19, 21, 24, 27, 31, 35, 40, 46, 52, 59, 67, 77, 87, 99, 113,
)


def nn(a, b):
    return lax.dot_general(a, b, (((1,), (0,)), ((), ())), preferred_element_type=F32)


def nt(a, b):
    return lax.dot_general(a, b, (((1,), (1,)), ((), ())), preferred_element_type=F32)


def tn(a, b):
    return lax.dot_general(a, b, (((0,), (0,)), ((), ())), preferred_element_type=F32)


def iota(shape, axis):
    return lax.broadcasted_iota(jnp.int32, shape, axis)


def rms(v, gain):
    return v * lax.rsqrt(jnp.mean(v * v, axis=-1, keepdims=True) + norm_epsilon) * gain


def rms_back(v, gain, e):
    s = lax.rsqrt(jnp.mean(v * v, axis=-1, keepdims=True) + norm_epsilon)
    eg = e * gain
    vs = v * s
    grad = s * (eg - vs * (s * jnp.mean(eg * v, axis=-1, keepdims=True)))
    return grad, jnp.sum(e * vs, axis=0, keepdims=True)


def gelu_cdf(x):
    return 0.5 * (1.0 + lax.erf(x * 0.7071067811865476))


def gelu_slope(x, cdf):
    return cdf + x * (0.3989422804014327 * jnp.exp(-0.5 * x * x))


class Refs:
    pass


class Group:
    def __init__(self, r, rows, fast):
        self.r = r
        self.rows = rows
        self.fast = fast
        self.t = lax.axis_index("tok")
        self.f = lax.axis_index("ffn")
        self.c = self.f % 2
        self.sib = self.f + 1 - 2 * self.c
        self.cross = (self.f + 2) % GROUP
        self.diag = (self.sib + 2) % GROUP
        self.near = (self.f // 2) * (2 * rows)
        self.far = 2 * rows - self.near
        self.y = self.t % 2
        self.z = self.t // 2
        self.y_peer = (self.t + 1 - 2 * self.y, self.f)
        self.z_peers = [(((self.z + k + 1) % 4) * 2 + self.y, self.f) for k in range(3)]
        self.count = 0
        self.local = 0

    def slot(self, index):
        return pl.ds(pl.multiple_of(index * self.rows, 32), self.rows)

    def near_rows(self):
        return pl.ds(pl.multiple_of(self.near, 64), 2 * self.rows)

    def far_rows(self):
        return pl.ds(pl.multiple_of(self.far, 64), 2 * self.rows)

    def others(self, tok):
        found = [(self.t, other) for other in (self.sib, self.cross, self.diag)]
        return found + [self.y_peer] + self.z_peers if tok else found

    def signal(self, tok=False):
        barrier = pltpu.get_barrier_semaphore()
        for other in self.others(tok):
            pl.semaphore_signal(barrier, inc=1, device_id=other, device_id_type=MESH)

    def wait(self, tok=False):
        pl.semaphore_wait(pltpu.get_barrier_semaphore(), len(self.others(tok)))

    def copy_to(self, src, dst, device):
        k = self.count
        self.count += 1
        return pltpu.make_async_remote_copy(
            src_ref=src,
            dst_ref=dst,
            send_sem=self.r.send.at[k],
            recv_sem=self.r.recv.at[k],
            device_id=device,
            device_id_type=MESH,
        )

    def copy(self, src, dst, other):
        return self.copy_to(src, dst, (self.t, other))

    def move(self, src, dst):
        k = self.local
        self.local += 1
        moving = pltpu.make_async_copy(src, dst, self.r.local.at[k])
        moving.start()
        return moving


class Gather:
    def __init__(self, g, ref):
        self.g, self.ref = g, ref
        own = ref.at[g.slot(g.f), :]
        self.x = g.copy(own, own, g.cross)
        self.s = g.copy(own, own, g.sib)
        got = ref.at[g.slot(g.cross), :]
        self.h = g.copy(got, got, g.sib)

    def start(self):
        self.x.start()
        self.s.start()

    def near(self):
        self.s.wait_recv()

    def relay(self):
        self.x.wait_recv()
        self.h.start()

    def far(self):
        self.h.wait_recv()

    def done(self):
        self.x.wait_send()
        self.s.wait_send()
        self.h.wait_send()


class Scatter:
    def __init__(self, g, r, work, got):
        self.g = g
        self.near_f32 = getattr(r, work + "_near")
        self.far_low = getattr(r, work + "_far")
        self.sib_low = getattr(r, work + "_sib")
        self.sum_low = getattr(r, work + "_sum")
        self.got = getattr(r, got + "_got")
        self.a = g.copy(self.far_low.at[1 - g.c], self.got.at[0], g.sib)
        self.b = g.copy(self.sib_low, self.got.at[1], g.sib)
        self.x = g.copy(self.sum_low, self.got.at[2], g.cross)

    def put_far(self, value):
        rows = self.g.rows
        low = value.astype(BF)
        self.far_low[0] = low[:rows]
        self.far_low[1] = low[rows:]
        self.a.start()

    def put_near(self, value):
        rows = self.g.rows
        self.near_f32[0] = value[:rows]
        self.near_f32[1] = value[rows:]
        self.sib_low[...] = self.near_f32[1 - self.g.c].astype(BF)
        self.b.start()

    def relay(self):
        self.a.wait_recv()
        total = self.got[0].astype(F32) + self.far_low[self.g.c].astype(F32)
        self.sum_low[...] = total.astype(BF)
        self.x.start()

    def result(self):
        self.b.wait_recv()
        part = self.near_f32[self.g.c] + self.got[1].astype(F32)
        self.x.wait_recv()
        return part + self.got[2].astype(F32)

    def done(self):
        self.a.wait_send()
        self.b.wait_send()
        self.x.wait_send()


def work_scratch(tag, rows, width):
    return {
        tag + "_near": ((2, rows, width), F32),
        tag + "_far": ((2, rows, width), BF),
        tag + "_sib": ((rows, width), BF),
        tag + "_sum": ((rows, width), BF),
    }


class Exchange:
    def __init__(self, g, src, dst):
        self.g, self.src, self.dst = g, src, dst
        self.diag, self.cross, self.sib = [
            g.copy(src.at[g.slot(other), :], dst.at[g.f], other)
            for other in (g.diag, g.cross, g.sib)
        ]

    def start_far(self):
        self.diag.start()
        self.cross.start()

    def start_near(self):
        self.sib.start()
        self.dst[self.g.f] = self.src[self.g.slot(self.g.f), :]

    def recv(self):
        for copy in (self.sib, self.cross, self.diag):
            copy.wait_recv()

    def done(self):
        for copy in (self.sib, self.cross, self.diag):
            copy.wait_send()


class TokSum:
    def __init__(self, g, unit, y_got, z_got, out):
        self.g, self.unit, self.y_got, self.z_got, self.out = g, unit, y_got, z_got, out
        if not g.fast:
            return
        self.y = g.copy_to(unit.at[1 - g.y], y_got, g.y_peer)
        self.zs = [
            g.copy_to(unit.at[g.y, (g.z + k + 1) % 4], z_got.at[k], peer)
            for k, peer in enumerate(g.z_peers)
        ]

    def put(self, value, first=0):
        width = value.shape[1]
        low = value.astype(BF)
        if not self.g.fast:
            self.out[:, first : first + width] = low
            return
        share = self.unit.shape[2]
        for t in range(8):
            self.unit[t % 2, t // 2, :, first : first + width] = low[t * share : (t + 1) * share]

    def start(self):
        if self.g.fast:
            self.y.start()

    def turn(self):
        if not self.g.fast:
            return
        y = self.g.y
        self.y.wait_recv()
        self.y.wait_send()
        self.unit[y] = (self.unit[y].astype(F32) + self.y_got[...].astype(F32)).astype(BF)
        for copy in self.zs:
            copy.start()

    def finish(self):
        if not self.g.fast:
            return
        total = self.unit[self.g.y, self.g.z].astype(F32)
        for k, copy in enumerate(self.zs):
            copy.wait_recv()
            total = total + self.z_got[k].astype(F32)
        self.out[...] = total
        for copy in self.zs:
            copy.wait_send()


class SmallSum:
    def __init__(self, g, pairs):
        self.g, self.pairs = g, pairs
        if not g.fast:
            return
        self.steps = [[], [], []]
        for own, in_group, in_y, in_z, out in pairs:
            for other in (g.sib, g.cross, g.diag):
                self.steps[0].append(g.copy(in_group.at[g.f], in_group.at[g.f], other))
            self.steps[1].append(g.copy_to(in_y.at[g.y], in_y.at[g.y], g.y_peer))
            for peer in g.z_peers:
                self.steps[2].append(g.copy_to(in_z.at[g.z], in_z.at[g.z], peer))

    def begin(self):
        if not self.g.fast:
            for own, _, _, _, out in self.pairs:
                out[...] = own[...]
            return
        for own, in_group, _, _, _ in self.pairs:
            in_group[self.g.f] = own[...]
        self.go(0)

    def go(self, step):
        for copy in self.steps[step]:
            copy.start()

    def end(self, step):
        for copy in self.steps[step]:
            copy.wait_recv()
        for copy in self.steps[step]:
            copy.wait_send()

    def second(self):
        if not self.g.fast:
            return
        self.end(0)
        for _, in_group, in_y, _, _ in self.pairs:
            in_y[self.g.y] = in_group[0] + in_group[1] + in_group[2] + in_group[3]
        self.go(1)

    def third(self):
        if not self.g.fast:
            return
        self.end(1)
        for _, _, in_y, in_z, _ in self.pairs:
            in_z[self.g.z] = in_y[0] + in_y[1]
        self.go(2)

    def finish(self):
        if not self.g.fast:
            return
        self.end(2)
        for _, _, _, in_z, out in self.pairs:
            out[...] = in_z[0] + in_z[1] + in_z[2] + in_z[3]


def merged_out(dst, w_out):
    width = dst.shape[2]
    total = nn(dst[0], w_out[:width, :])
    for p in range(1, GROUP):
        total = total + nn(dst[p], w_out[p * width : (p + 1) * width, :])
    return total


def run(name, cid, body, ins, outs, scratch, counts, rows, fast):
    in_names, out_names, scr_names = list(ins), list(outs), list(scratch)

    def kernel(*refs):
        r = Refs()
        for n, ref in zip(in_names + out_names + scr_names + ["send", "recv", "local"], refs):
            setattr(r, n, ref)
        body(r, Group(r, rows, fast))

    spaces = {"v": pltpu.VMEM, "s": pltpu.SMEM, "h": pl.ANY}
    got = pl.pallas_call(
        kernel,
        out_shape=[jax.ShapeDtypeStruct(*outs[n][:2]) for n in out_names],
        in_specs=[pl.BlockSpec(memory_space=spaces[ins[n][1]]) for n in in_names],
        out_specs=[pl.BlockSpec(memory_space=spaces[outs[n][2]]) for n in out_names],
        scratch_shapes=[pltpu.VMEM(*scratch[n]) for n in scr_names]
        + [
            pltpu.SemaphoreType.DMA((counts[0],)),
            pltpu.SemaphoreType.DMA((counts[0],)),
            pltpu.SemaphoreType.DMA((counts[1],)),
        ],
        compiler_params=pltpu.CompilerParams(
            collective_id=cid, has_side_effects=True, vmem_limit_bytes=VMEM_LIMIT
        ),
        name=name,
    )(*[ins[n][0] for n in in_names])
    return dict(zip(out_names, got))


TILE = 64


def segment_starts(lens, count):
    starts = [jnp.int32(0)]
    for e in range(count - 1):
        starts.append(starts[-1] + lens[0, e])
    return starts


def segment_of(place, starts):
    total = jnp.zeros(place.shape, jnp.int32)
    for s in starts[1:]:
        total = total + (place >= s).astype(jnp.int32)
    return total


def enc_bias_tiles(tables, out, f, heads):
    shape = (TILE, SLOT)
    r = iota(shape, 1) - iota(shape, 0)
    for d in range(-4, 4):
        least, most = TILE * d - (TILE - 1), TILE * d + SLOT - 1

        def entry(bucket, h):
            return tables[0, bucket, f * heads + h]

        if least > 0:
            first = 16 + sum(limit <= least for limit in wide_limits)
        elif most < 0:
            first = sum(limit <= -most for limit in wide_limits)
        else:
            first = 0
        values = [jnp.full(shape, entry(first, h), F32) for h in range(heads)]
        rel = r + TILE * d
        for b, limit in enumerate(wide_limits):
            if least < limit <= most:
                hit = rel >= limit
                values = [jnp.where(hit, entry(17 + b, h), values[h]) for h in range(heads)]
            if least <= -limit < most:
                hit = rel <= -limit
                values = [jnp.where(hit, entry(1 + b, h), values[h]) for h in range(heads)]
        for h in range(heads):
            out[h, d + 4] = values[h]


def dec_bias_block(tables, out, f, heads):
    side = SLOT
    m = iota((side, side), 0) - iota((side, side), 1)
    values = [jnp.full((side, side), tables[1, 0, f * heads + h], F32) for h in range(heads)]
    for b, limit in enumerate(causal_limits):
        hit = m >= limit
        values = [jnp.where(hit, tables[1, 1 + b, f * heads + h], values[h]) for h in range(heads)]
    for h in range(heads):
        out[h] = values[h]


def put_heads(g, ref, rows, value, first, heads):
    window = (heads + 1) * DH
    for w in range(value.shape[1] // window):
        part = pltpu.roll(value[:, w * window : (w + 1) * window], heads * DH * g.c, 1).astype(BF)
        for h in range(heads):
            ref[first + w * heads + h, rows, :] = part[:, h * DH : (h + 1) * DH]


def put_grads(g, grads, windows, rows, index, values):
    heads = len(values)
    window = (heads + 1) * DH
    whole = jnp.concatenate(values + [jnp.zeros_like(values[0])], axis=1)
    low = whole.astype(BF)
    grads[rows, index * heads * DH : (index + 1) * heads * DH] = low[:, : heads * DH]
    windows[rows, index * window : (index + 1) * window] = pltpu.roll(whole, DH * g.c, 1).astype(BF)


def softmax_low(scores):
    top = jnp.max(scores, axis=-1, keepdims=True)
    raised = jnp.exp(scores - top)
    return (raised * (1.0 / jnp.sum(raised, axis=-1, keepdims=True))).astype(BF)


def half_attend(qkv, probs, mixed, base, count, heads, packed, scores_of):
    rows = pl.ds(pl.multiple_of(base, TILE), count)
    scores = [nt(qkv[h, rows, :], qkv[heads + h]) for h in range(heads)]
    lows = []
    for h in range(heads):
        parts = [
            softmax_low(scores_of(h, i, scores[h][i * TILE : (i + 1) * TILE]))
            for i in range(count // TILE)
        ]
        lows.append(jnp.concatenate(parts, axis=0))
        probs[h, rows, :] = lows[h]
    for h in range(heads):
        mixed[rows, h * DH : (h + 1) * DH] = nn(lows[h], qkv[2 * heads + h]).astype(BF)


def enc_attend(qkv, probs, mixed, bias, starts, base, count, heads, packed):
    seg_keys = segment_of(iota((1, packed), 1), starts)
    place = iota((TILE, 1), 0)

    def scores_of(h, i, scores):
        seg_rows = segment_of(place + (base + i * TILE), starts)
        first = -i - base // TILE
        add = jnp.concatenate(
            [bias[h, jnp.clip(2 * j + first, -4, 3) + 4] for j in range(packed // SLOT)], axis=1
        )
        return jnp.where(seg_rows == seg_keys, scores + add, masked_score)

    half_attend(qkv, probs, mixed, base, count, heads, packed, scores_of)


def cross_attend(qkv, probs, mixed, starts, base, count, heads, packed):
    seg_keys = segment_of(iota((1, packed), 1), starts)

    def scores_of(h, i, scores):
        slot = (base // TILE + i) // (SLOT // TILE)
        return jnp.where(seg_keys == slot, scores, masked_score)

    half_attend(qkv, probs, mixed, base, count, heads, packed, scores_of)


def self_attend(qkv, probs, mixed, bias, lens, heads, packed):
    place = iota((SLOT, SLOT), 1)
    lower = place <= iota((SLOT, SLOT), 0)
    pairs = [(i, h, slice(i * SLOT, (i + 1) * SLOT)) for i in range(packed // SLOT) for h in range(heads)]
    scores = [nt(qkv[h, rows, :], qkv[heads + h, rows, :]) for i, h, rows in pairs]
    lows = []
    for (i, h, rows), value in zip(pairs, scores):
        live = lower & (place < lens[0, i])
        lows.append(softmax_low(jnp.where(live, value + bias[h], masked_score)))
    for (i, h, rows), low in zip(pairs, lows):
        probs[h, rows, :] = low
        mixed[rows, h * DH : (h + 1) * DH] = nn(low, qkv[2 * heads + h, rows, :]).astype(BF)


def full_attend_back(g, qkv, probs, grad_mixed, grads, windows, heads, packed, half):
    every = slice(0, packed)
    mixes = [grad_mixed[:, h * DH : (h + 1) * DH] for h in range(heads)]
    put_grads(g, grads, windows, every, 2, [tn(probs[h], mixes[h]) for h in range(heads)])
    for part in range(packed // half):
        rows = slice(part * half, (part + 1) * half)
        passed = [nt(mixes[h][rows], qkv[2 * heads + h]) for h in range(heads)]
        lows = []
        for h in range(heads):
            weights = probs[h, rows, :].astype(F32)
            product = weights * passed[h]
            lows.append((product - weights * jnp.sum(product, axis=-1, keepdims=True)).astype(BF))
            probs[h, rows, :] = lows[h]
        put_grads(g, grads, windows, rows, 0, [nn(lows[h], qkv[heads + h]) for h in range(heads)])
    put_grads(g, grads, windows, every, 1, [tn(probs[h], qkv[h]) for h in range(heads)])


def self_attend_back(g, qkv, probs, grad_mixed, ds_sum, grads, windows, heads, packed):
    blocks = packed // SLOT
    pairs = [(i, h, slice(i * SLOT, (i + 1) * SLOT)) for i in range(blocks) for h in range(heads)]
    mixes = [grad_mixed[rows, h * DH : (h + 1) * DH] for i, h, rows in pairs]
    passed = [nt(mix, qkv[2 * heads + h, rows, :]) for (i, h, rows), mix in zip(pairs, mixes)]
    wides = []
    for (i, h, rows), value in zip(pairs, passed):
        weights = probs[h, rows, :].astype(F32)
        product = weights * value
        wides.append(product - weights * jnp.sum(product, axis=-1, keepdims=True))
    for h in range(heads):
        total = wides[h]
        for i in range(1, blocks):
            total = total + wides[i * heads + h]
        ds_sum[h] = total
    lows = [value.astype(BF) for value in wides]
    for i in range(blocks):
        rows = slice(i * SLOT, (i + 1) * SLOT)
        own = range(i * heads, (i + 1) * heads)
        put_grads(g, grads, windows, rows, 0, [nn(lows[n], qkv[heads + n % heads, rows, :]) for n in own])
        put_grads(g, grads, windows, rows, 1, [tn(lows[n], qkv[n % heads, rows, :]) for n in own])
        put_grads(g, grads, windows, rows, 2, [tn(probs[n % heads, rows, :], mixes[n]) for n in own])


def put_table(out, first, lines, f, heads):
    lane = iota((BUCKETS, 128), 1)
    total = jnp.zeros((BUCKETS, 128), F32)
    for h in range(heads):
        summed = jnp.sum(lines[h], axis=1, keepdims=True)
        total = jnp.where(lane == f * heads + h, summed, total)
    out[first : first + BUCKETS, :] = total


def dec_table_grad(ds_sum, line, out, first, f, heads):
    m = iota((SLOT, SLOT), 0) - iota((SLOT, SLOT), 1)
    limits = (0,) + causal_limits + (SLOT,)
    for b in range(BUCKETS):
        hit = (m >= limits[b]) & (m < limits[b + 1]) if b else m <= 0
        for h in range(heads):
            line[h, b : b + 1, :] = jnp.sum(
                jnp.where(hit, ds_sum[h], 0.0), axis=0, keepdims=True
            )
    put_table(out, first, [line[h] for h in range(heads)], f, heads)


def enc_table_grad(ds, ds_sum, line, out, first, f, heads, packed):
    blocks = packed // SLOT
    r = iota((SLOT, SLOT), 1) - iota((SLOT, SLOT), 0)
    limits = wide_limits + (10**6,)
    for h in range(heads):
        for slot in range(5):
            total = jnp.zeros((SLOT, SLOT), F32)
            for i in range(blocks):
                for j in range(blocks):
                    if max(-2, min(2, j - i)) == slot - 2:
                        total = total + ds[h, i * SLOT : (i + 1) * SLOT, j * SLOT : (j + 1) * SLOT].astype(F32)
            ds_sum[h, slot] = total
    for h in range(heads):
        line[h] = jnp.zeros((BUCKETS, SLOT), F32)
        line[h, 0:1, :] = jnp.sum(jnp.where(r == 0, ds_sum[h, 2], 0.0), axis=0, keepdims=True)
    for b in range(15):
        low, high = limits[b], limits[b + 1]
        for side in (1, -1):
            rel = side * r
            hit_same = (rel >= low) & (rel < high)
            hit_next = (rel + SLOT >= low) & (rel + SLOT < high)
            row = 1 + b + (16 if side > 0 else 0)
            for h in range(heads):
                total = jnp.where(hit_same, ds_sum[h, 2], 0.0) + jnp.where(
                    hit_next, ds_sum[h, 2 + side], 0.0
                )
                if b == 14:
                    total = total + ds_sum[h, 2 + 2 * side]
                line[h, row : row + 1, :] = jnp.sum(total, axis=0, keepdims=True)
    put_table(out, first, [line[h] for h in range(heads)], f, heads)


def load_windows(g, w, layer, qk_weights, v_weights, window):
    width = window - DH
    first = pl.ds(pl.multiple_of(((g.f * width) // 128) * 128, 128), window)
    return [
        g.move(qk_weights.at[layer, 0, :, first], w.at[:, :window]),
        g.move(qk_weights.at[layer, 1, :, first], w.at[:, window : 2 * window]),
        g.move(v_weights.at[layer, :, first], w.at[:, 2 * window :]),
    ]


def wait_all(items):
    for item in items:
        item.wait()


def forward(r, g):
    rows, f = g.rows, g.f
    packed = GROUP * rows
    half = 2 * rows
    heads = r.qkv_e.shape[0] // 3
    window = (heads + 1) * DH
    own, near, far = g.slot(f), g.near_rows(), g.far_rows()
    g.signal()
    get_e = load_windows(g, r.w_e, 0, r.qk_weights, r.v_weights, window)
    get_oe = g.move(r.out_weights.at[0], r.wo_e)
    get_d = load_windows(g, r.w_d, 1, r.qk_weights, r.v_weights, window)
    get_od = g.move(r.out_weights.at[1], r.wo_d)
    get_in = g.move(r.ffn_in.at[0], r.w_in)
    get_down = g.move(r.ffn_out.at[0], r.w_down)
    get_c = load_windows(g, r.w_c, 2, r.qk_weights, r.v_weights, window)
    get_oc = g.move(r.out_weights.at[2], r.wo_c)
    stores = []

    def keep(*names):
        for n in names:
            stores.append(g.move(getattr(r, n), getattr(r, "out_" + n)))

    ga, gb, gc, gd, gm, gg = [
        Gather(g, ref) for ref in (r.gath_a, r.gath_b, r.gath_c, r.gath_d, r.gath_m, r.gath_g)
    ]
    xe, xd, xc = [
        Exchange(g, *pair)
        for pair in ((r.mixed_e, r.merged_e), (r.mixed_d, r.merged_d), (r.mixed_c, r.merged_c))
    ]
    rs = Scatter(g, r, "wa", "ra")
    r.gath_a[own, :] = rms(r.enc_in[...].astype(F32), r.gains[0:1, :]).astype(BF)
    g.wait()
    ga.start()
    r.gath_c[own, :] = rms(r.dec_in[...].astype(F32), r.gains[3:4, :]).astype(BF)
    r.gath_g[own, :] = r.cot[...]
    enc_bias_tiles(r.tables, r.bias_e, f, heads)
    dec_bias_block(r.tables, r.bias_d, f, heads)
    starts = segment_starts(r.enc_lens, packed // SLOT)
    wait_all(get_e)
    ga.near()
    put_heads(g, r.qkv_e, near, nn(r.gath_a[near, :], r.w_e[...]), 0, heads)
    ga.relay()
    gc.start()
    ga.far()
    put_heads(g, r.qkv_e, far, nn(r.gath_a[far, :], r.w_e[...]), 0, heads)
    enc_attend(r.qkv_e, r.probs_e, r.mixed_e, r.bias_e, starts, g.far, half, heads, packed)
    xe.start_far()
    enc_attend(r.qkv_e, r.probs_e, r.mixed_e, r.bias_e, starts, g.near, half, heads, packed)
    xe.start_near()
    keep("gath_a", "qkv_e", "probs_e", "mixed_e")
    get_oe.wait()
    xe.recv()
    x1 = r.enc_in[...].astype(F32) + merged_out(r.merged_e, r.wo_e)
    r.x1[...] = x1
    r.gath_b[own, :] = rms(x1, r.gains[1:2, :]).astype(BF)
    gb.start()
    keep("x1")

    wait_all(get_d)
    gc.near()
    put_heads(g, r.qkv_d, near, nn(r.gath_c[near, :], r.w_d[...]), 0, heads)
    gc.relay()
    gc.far()
    put_heads(g, r.qkv_d, far, nn(r.gath_c[far, :], r.w_d[...]), 0, heads)

    def hidden_of(part):
        pre = nn(r.gath_b[part, :], r.w_in[...])
        cdf = gelu_cdf(pre)
        r.hidden0[part, :] = (pre * cdf).astype(BF)
        r.slope0[part, :] = gelu_slope(pre, cdf).astype(BF)

    get_in.wait()
    get_down.wait()
    gb.near()
    hidden_of(near)
    gb.relay()
    gb.far()
    hidden_of(far)
    rs.put_far(nn(r.hidden0[far, :], r.w_down[...]))
    rs.put_near(nn(r.hidden0[near, :], r.w_down[...]))
    rs.relay()
    keep("gath_b", "gath_c", "hidden0", "slope0")
    self_attend(r.qkv_d, r.probs_d, r.mixed_d, r.bias_d, r.dec_lens, heads, packed)
    xd.start_far()
    xd.start_near()
    keep("qkv_d", "probs_d", "mixed_d")
    x2 = r.x1[...] + rs.result()
    r.x2[...] = x2
    r.gath_m[own, :] = rms(x2, r.gains[2:3, :]).astype(BF)
    gm.start()
    keep("x2")
    get_od.wait()
    xd.recv()
    d1 = r.dec_in[...].astype(F32) + merged_out(r.merged_d, r.wo_d)
    r.d1[...] = d1
    r.gath_d[own, :] = rms(d1, r.gains[4:5, :]).astype(BF)
    gd.start()
    keep("d1")
    wait_all(get_c)
    gm.near()
    put_heads(g, r.qkv_c, near, nn(r.gath_m[near, :], r.w_c[:, window:]), heads, heads)
    gm.relay()
    gg.start()
    gd.near()
    put_heads(g, r.qkv_c, near, nn(r.gath_d[near, :], r.w_c[:, :window]), 0, heads)
    gd.relay()
    gm.far()
    put_heads(g, r.qkv_c, far, nn(r.gath_m[far, :], r.w_c[:, window:]), heads, heads)
    gd.far()
    put_heads(g, r.qkv_c, far, nn(r.gath_d[far, :], r.w_c[:, :window]), 0, heads)
    cross_attend(r.qkv_c, r.probs_c, r.mixed_c, starts, g.far, half, heads, packed)
    xc.start_far()
    cross_attend(r.qkv_c, r.probs_c, r.mixed_c, starts, g.near, half, heads, packed)
    xc.start_near()
    keep("gath_m", "gath_d", "qkv_c", "probs_c", "mixed_c")
    gg.relay()
    gg.near()
    gg.far()
    keep("gath_g")
    get_oc.wait()
    xc.recv()
    r.d2[...] = r.d1[...] + merged_out(r.merged_c, r.wo_c)
    keep("d2")
    for item in (ga, gb, gc, gd, gm, gg, xe, xd, xc, rs):
        item.done()
    wait_all(stores)


def backward(r, g):
    rows, f = g.rows, g.f
    packed = GROUP * rows
    half = 2 * rows
    heads = r.qkv_e.shape[0] // 3
    width = heads * DH
    window = width + DH
    own, near, far = g.slot(f), g.near_rows(), g.far_rows()
    g.signal(g.fast)

    def load(*names):
        return [g.move(getattr(r, "in_" + n), getattr(r, n)) for n in names]

    def part_of(layer):
        return r.out_weights.at[layer, pl.ds(pl.multiple_of(f * width, 32), width), :]

    get_d2 = load("d2")
    get_g = load("gath_g")
    get_ffn1 = [g.move(r.ffn_out.at[1], r.w_down), g.move(r.ffn_in.at[1], r.w_in)]
    get_cross = load("qkv_c", "probs_c", "mixed_c", "gath_d", "gath_m") + [g.move(part_of(2), r.wo_c)]
    get_cross += load_windows(g, r.w_c, 2, r.qk_weights, r.v_weights, window) + load("x2", "d1")
    get_ffn0 = load("hidden0", "slope0", "gath_b", "x1")
    get_self = load("qkv_d", "probs_d", "mixed_d", "gath_c") + [g.move(part_of(1), r.wo_d)]
    get_self += load_windows(g, r.w_d, 1, r.qk_weights, r.v_weights, window)
    get_enc = load("qkv_e", "probs_e", "mixed_e", "gath_a") + [g.move(part_of(0), r.wo_e)]
    get_enc += load_windows(g, r.w_e, 0, r.qk_weights, r.v_weights, window)

    ge, g2, gl, g1, gm = [
        Gather(g, ref) for ref in (r.gath_e, r.gath_g2, r.gath_g, r.gath_g1, r.gath_e)
    ]
    sb, sf, sm, sq, s0, sd, se = [
        Scatter(g, r, work, got)
        for work, got in (
            ("wa", "ra"), ("wb", "rb"), ("wa", "rc"), ("wb", "rd"), ("wa", "ra"), ("wb", "rb"), ("wa", "rc"),
        )
    ]
    units = [
        TokSum(g, getattr(r, "unit" + u), getattr(r, "ygot" + str(n)), getattr(r, "zgot" + str(n)), getattr(r, "sum" + str(n)))
        for n, u in enumerate("01230145")
    ] if g.fast else [TokSum(g, None, None, None, getattr(r, "sum" + str(n))) for n in range(8)]
    u_in1, u_down1, u_cross, u_self, u_in0, u_down0, u_vo, u_qk = units
    pairs = [
        (r.small_gain, r.gain_group, r.gain_y, r.gain_z, r.gain_sum),
        (r.small_table, r.table_group, r.table_y, r.table_z, r.table_sum),
    ] if g.fast else [
        (r.small_gain, None, None, None, r.gain_sum), (r.small_table, None, None, None, r.table_sum)
    ]
    small = SmallSum(g, pairs)

    wait_all(get_d2)
    r.gath_e[own, :] = rms(r.d2[...], r.gains[5:6, :]).astype(BF)
    r.small_gain[...] = jnp.zeros_like(r.small_gain)
    g.wait(g.fast)
    ge.start()
    wait_all(get_g)
    wait_all(get_ffn1)
    r.pre1[near, :] = nt(r.gath_g[near, :], r.w_down[...]).astype(BF)
    r.pre1[far, :] = nt(r.gath_g[far, :], r.w_down[...]).astype(BF)

    def backward_of(part):
        pre = nn(r.gath_e[part, :], r.w_in[...])
        cdf = gelu_cdf(pre)
        r.hidden1[part, :] = (pre * cdf).astype(BF)
        r.pre1[part, :] = (r.pre1[part, :].astype(F32) * gelu_slope(pre, cdf)).astype(BF)

    ge.near()
    backward_of(near)
    ge.relay()
    ge.far()
    backward_of(far)
    sb.put_far(nt(r.pre1[far, :], r.w_in[...]))
    sb.put_near(nt(r.pre1[near, :], r.w_in[...]))
    sb.relay()
    u_down1.put(tn(r.gath_g[...], r.hidden1[...]))
    u_down1.start()
    u_in1.put(tn(r.gath_e[...], r.pre1[...]))
    u_in1.start()
    sf.put_far(nn(r.hidden1[far, :], r.w_down[...]))
    sf.put_near(nn(r.hidden1[near, :], r.w_down[...]))
    d2 = r.d2[...]
    grad, gain = rms_back(d2, r.gains[5:6, :], sb.result())
    g2_value = r.cot[...].astype(F32) + grad
    r.gath_g2[own, :] = g2_value.astype(BF)
    ge.done()
    g2.start()
    r.g2[...] = g2_value
    r.small_gain[5:6, :] = gain
    get_ffn0 += [g.move(r.ffn_in.at[0], r.w_in), g.move(r.ffn_out.at[0], r.w_down)]

    wait_all(get_cross)
    g2.near()
    r.gmix[near, :] = nt(r.gath_g2[near, :], r.wo_c[...]).astype(BF)
    g2.relay()
    sf.relay()
    g2.far()
    r.gmix[far, :] = nt(r.gath_g2[far, :], r.wo_c[...]).astype(BF)
    full_attend_back(g, r.qkv_c, r.probs_c, r.gmix, r.grads, r.gwin, heads, packed, half)
    sb.done()
    sm.put_far(nt(r.gwin[far, window:], r.w_c[:, window:]))
    sm.put_near(nt(r.gwin[near, window:], r.w_c[:, window:]))
    sm.relay()
    r.dec_out[...] = (d2 + sf.result()).astype(BF)
    sf.done()
    sq.put_far(nt(r.gwin[far, :window], r.w_c[:, :window]))
    sq.put_near(nt(r.gwin[near, :window], r.w_c[:, :window]))
    u_down1.turn()
    u_in1.turn()
    u_cross.put(tn(r.gath_d[...], r.grads[:, :width]), 0)
    u_cross.put(tn(r.gath_m[...], r.grads[:, width:]), width)
    u_cross.put(tn(r.gath_g2[...], r.mixed_c[...]), 3 * width)
    u_cross.start()
    grad, gain = rms_back(r.x2[...], r.gains[2:3, :], sm.result())
    r.gath_g[own, :] = grad.astype(BF)
    gl.start()
    r.x2[...] = grad
    r.small_gain[2:3, :] = gain

    wait_all(get_ffn0)

    def back_of(part):
        back = nt(r.gath_g[part, :], r.w_down[...]).astype(BF).astype(F32) * r.slope0[part, :].astype(F32)
        r.slope0[part, :] = back.astype(BF)

    gl.near()
    back_of(near)
    gl.relay()
    sq.relay()
    gl.far()
    back_of(far)
    sm.done()
    s0.put_far(nt(r.slope0[far, :], r.w_in[...]))
    s0.put_near(nt(r.slope0[near, :], r.w_in[...]))
    s0.relay()
    grad, gain = rms_back(r.d1[...], r.gains[4:5, :], sq.result())
    g1_value = r.g2[...] + grad
    r.gath_g1[own, :] = g1_value.astype(BF)
    g1.start()
    r.d1[...] = g1_value
    r.small_gain[4:5, :] = gain
    u_down1.finish()
    u_in1.finish()
    u_down0.put(tn(r.gath_g[...], r.hidden0[...]))
    u_down0.start()
    u_in0.put(tn(r.gath_b[...], r.slope0[...]))
    u_in0.start()
    u_cross.turn()
    grad, gain = rms_back(r.x1[...], r.gains[1:2, :], s0.result())
    gm_value = r.x2[...] + grad
    r.gath_e[own, :] = gm_value.astype(BF)
    gm.start()
    r.x2[...] = gm_value
    r.small_gain[1:2, :] = gain

    wait_all(get_self)
    sq.done()
    g1.near()
    r.gmix[near, :] = nt(r.gath_g1[near, :], r.wo_d[...]).astype(BF)
    g1.relay()
    g1.far()
    r.gmix[far, :] = nt(r.gath_g1[far, :], r.wo_d[...]).astype(BF)
    self_attend_back(g, r.qkv_d, r.probs_d, r.gmix, r.ds_self, r.grads, r.gwin, heads, packed)
    sd.put_far(nt(r.gwin[far, :], r.w_d[...]))
    sd.put_near(nt(r.gwin[near, :], r.w_d[...]))
    u_self.put(tn(r.gath_c[...], r.grads[...]), 0)
    u_self.put(tn(r.gath_g1[...], r.mixed_d[...]), 3 * width)
    u_self.start()

    wait_all(get_enc)
    gm.near()
    r.gmix[near, :] = nt(r.gath_e[near, :], r.wo_e[...]).astype(BF)
    gm.relay()
    sd.relay()
    gm.far()
    r.gmix[far, :] = nt(r.gath_e[far, :], r.wo_e[...]).astype(BF)
    full_attend_back(g, r.qkv_e, r.probs_e, r.gmix, r.grads, r.gwin, heads, packed, half)
    s0.done()
    se.put_far(nt(r.gwin[far, :], r.w_e[...]))
    se.put_near(nt(r.gwin[near, :], r.w_e[...]))
    se.relay()
    u_qk.put(tn(r.gath_a[...], r.grads[:, : 2 * width]), 0)
    u_qk.start()
    u_vo.put(tn(r.gath_a[...], r.grads[:, 2 * width :]), 0)
    u_vo.put(tn(r.gath_e[...], r.mixed_e[...]), width)
    u_vo.start()
    u_down0.turn()
    u_in0.turn()
    dec_table_grad(r.ds_self, r.line, r.small_table, BUCKETS, f, heads)
    enc_table_grad(r.probs_e, r.ds_enc, r.line, r.small_table, 0, f, heads, packed)
    grad, gain = rms_back(r.dec_in[...].astype(F32), r.gains[3:4, :], sd.result())
    r.dec_grad[...] = (r.d1[...] + grad).astype(BF)
    r.small_gain[3:4, :] = gain
    grad, gain = rms_back(r.enc_in[...].astype(F32), r.gains[0:1, :], se.result())
    r.enc_grad[...] = (r.x2[...] + grad).astype(BF)
    r.small_gain[0:1, :] = gain
    small.begin()
    u_self.turn()
    u_qk.turn()
    small.second()
    u_vo.turn()
    u_cross.finish()
    u_down0.finish()
    small.third()
    u_in0.finish()
    u_self.finish()
    small.finish()
    u_qk.finish()
    u_vo.finish()
    for item in (g2, gl, g1, gm, sd, se):
        item.done()


def layout(r):
    width = r.qk.shape[3]
    for name in ("dec_out", "enc_grad", "dec_grad"):
        getattr(r, "out_" + name)[...] = getattr(r, name)[...]
    r.up[0] = r.sum4[...]
    r.up[1] = r.sum0[...]
    r.down[0] = r.sum5[...].T
    r.down[1] = r.sum1[...].T
    for layer, part in ((1, r.sum3), (2, r.sum2)):
        r.qk[layer, 0] = part[:, :width]
        r.qk[layer, 1] = part[:, width : 2 * width]
        r.v[layer] = part[:, 2 * width : 3 * width]
        r.o[layer] = part[:, 3 * width :].T
    r.qk[0, 0] = r.sum7[:, :width]
    r.qk[0, 1] = r.sum7[:, width:]
    r.v[0] = r.sum6[:, :width]
    r.o[0] = r.sum6[:, width:].T
    r.table[0] = r.table_sum[:BUCKETS, : r.table.shape[2]]
    r.table[1] = r.table_sum[BUCKETS:, : r.table.shape[2]]
    r.gain[...] = r.gain_sum[:6, :]
    r.final[...] = r.gain_sum[5:6, :]


def on_device(
    enc_in,
    dec_in,
    cotangent,
    enc_lengths,
    dec_lengths,
    qk_weights,
    v_weights,
    out_weights,
    ffn_in,
    ffn_out,
    bias_tables,
    gains,
):
    group_size = lax.axis_size("ffn")
    tok_size = lax.axis_size("tok")
    fast = tok_size == 8
    rows, model = enc_in.shape
    packed = rows * group_size
    width = qk_weights.shape[3] // group_size
    heads = width // DH
    hidden = ffn_in.shape[2]
    side = SLOT
    share = model // tok_size
    total_heads = bias_tables.shape[2]

    low = lambda *shape: (shape, BF)
    wide = lambda *shape: (shape, F32)
    v = lambda a: (a, "v")
    s = lambda a: (a, "s")
    h = lambda a: (a, "h")

    kept = dict(
        gath_a=low(packed, model), gath_b=low(packed, model), gath_c=low(packed, model),
        gath_d=low(packed, model), gath_m=low(packed, model), gath_g=low(packed, model),
        qkv_e=low(3 * heads, packed, DH), qkv_d=low(3 * heads, packed, DH), qkv_c=low(3 * heads, packed, DH),
        probs_e=low(heads, packed, packed), probs_d=low(heads, packed, side), probs_c=low(heads, packed, packed),
        mixed_e=low(packed, width), mixed_d=low(packed, width), mixed_c=low(packed, width),
        hidden0=low(packed, hidden), slope0=low(packed, hidden),
        x1=wide(rows, model), x2=wide(rows, model), d1=wide(rows, model), d2=wide(rows, model),
    )
    weights = dict(
        w_e=low(model, 3 * (width + DH)), w_d=low(model, 3 * (width + DH)), w_c=low(model, 3 * (width + DH)),
        w_in=low(model, hidden), w_down=low(hidden, model),
    )
    a = run(
        "forward", 1, forward,
        dict(
            enc_in=v(enc_in), dec_in=v(dec_in), cot=v(cotangent), gains=v(gains), tables=s(bias_tables),
            enc_lens=s(enc_lengths), dec_lens=s(dec_lengths), qk_weights=h(qk_weights), v_weights=h(v_weights),
            out_weights=h(out_weights), ffn_in=h(ffn_in), ffn_out=h(ffn_out),
        ),
        {"out_" + n: kept[n] + ("h",) for n in kept},
        dict(
            kept,
            **weights,
            wo_e=low(model, model), wo_d=low(model, model), wo_c=low(model, model),
            bias_e=wide(heads, 8, TILE, side), bias_d=wide(heads, side, side),
            merged_e=low(GROUP, rows, width), merged_d=low(GROUP, rows, width), merged_c=low(GROUP, rows, width),
            ra_got=low(3, rows, model),
            **work_scratch("wa", rows, model),
        ),
        (30, 14 + len(kept)), rows, fast,
    )
    sums = [hidden, hidden, 4 * width, 4 * width, hidden, hidden, 2 * width, 2 * width]
    units = dict(zip("012345", (hidden, hidden, 4 * width, 4 * width, 2 * width, 2 * width)))
    tok_scratch = {}
    if fast:
        tok_scratch.update({"unit" + u: low(2, 4, share, w) for u, w in units.items()})
        for n, w in enumerate(sums):
            tok_scratch["ygot%d" % n] = low(4, share, w)
            tok_scratch["zgot%d" % n] = low(3, share, w)
        for tag, shape in (("gain", (8, model)), ("table", (2 * BUCKETS, 128))):
            tok_scratch[tag + "_group"] = wide(GROUP, *shape)
            tok_scratch[tag + "_y"] = wide(2, *shape)
            tok_scratch[tag + "_z"] = wide(4, *shape)
    b = run(
        "backward", 2, backward,
        dict(
            enc_in=v(enc_in), dec_in=v(dec_in), cot=v(cotangent), gains=v(gains), qk_weights=h(qk_weights),
            v_weights=h(v_weights), out_weights=h(out_weights), ffn_in=h(ffn_in), ffn_out=h(ffn_out),
            **{"in_" + n: h(a["out_" + n]) for n in kept},
        ),
        dict(
            dec_out=low(rows, model) + ("v",), enc_grad=low(rows, model) + ("v",), dec_grad=low(rows, model) + ("v",),
            gain_sum=wide(8, model) + ("v",), table_sum=wide(2 * BUCKETS, 128) + ("v",),
            **{
                "sum%d" % n: (wide(share, w) if fast else low(model, w)) + ("v",) for n, w in enumerate(sums)
            },
        ),
        dict(
            kept,
            **weights,
            wo_e=low(width, model), wo_d=low(width, model), wo_c=low(width, model),
            gath_e=low(packed, model), gath_g2=low(packed, model), gath_g1=low(packed, model),
            pre1=low(packed, hidden), hidden1=low(packed, hidden), gmix=low(packed, width),
            grads=low(packed, 3 * width), gwin=low(packed, 3 * (width + DH)), g2=wide(rows, model),
            ds_self=wide(heads, side, side), ds_enc=wide(heads, 5, side, side), line=wide(heads, BUCKETS, side),
            small_gain=wide(8, model), small_table=wide(2 * BUCKETS, 128),
            ra_got=low(3, rows, model), rb_got=low(3, rows, model), rc_got=low(3, rows, model),
            rd_got=low(3, rows, model),
            **work_scratch("wa", rows, model), **work_scratch("wb", rows, model),
            **tok_scratch,
        ),
        (36 + (32 + 14 if fast else 0), 19 + len(kept)), rows, fast,
    )
    names = ["dec_out", "enc_grad", "dec_grad", "gain_sum", "table_sum"] + ["sum%d" % n for n in range(8)]
    if not fast:
        for n in range(8):
            b["sum%d" % n] = lax.psum_scatter(
                b["sum%d" % n], "tok", scatter_dimension=0, tiled=True
            ).astype(F32)
        b["gain_sum"], b["table_sum"] = lax.psum((b["gain_sum"], b["table_sum"]), ("tok", "ffn"))
    if not fast:
        part = [b["sum%d" % n] for n in range(8)]
        cut = lambda u, n: u[:, n * width : (n + 1) * width]
        layers = [
            jnp.concatenate([part[7], part[6]], axis=1), part[3], part[2],
        ]
        return (
            b["dec_out"],
            b["enc_grad"],
            b["dec_grad"],
            jnp.stack([jnp.stack([cut(u, 0), cut(u, 1)]) for u in layers]),
            jnp.stack([cut(u, 2) for u in layers]),
            jnp.stack([cut(u, 3).T for u in layers]),
            jnp.stack([part[4], part[0]]),
            jnp.stack([part[5].T, part[1].T]),
            b["table_sum"].reshape(2, BUCKETS, 128)[:, :, :total_heads],
            b["gain_sum"][:6],
            b["gain_sum"][5],
        )
    outs = dict(
        out_dec_out=low(rows, model), out_enc_grad=low(rows, model), out_dec_grad=low(rows, model),
        qk=wide(3, 2, share, width), v=wide(3, share, width), o=wide(3, width, share),
        up=wide(2, share, hidden), down=wide(2, hidden, share), table=wide(2, BUCKETS, total_heads),
        gain=wide(6, model), final=wide(1, model),
    )

    def layout_kernel(*refs):
        r = Refs()
        for n, ref in zip(names + list(outs), refs):
            setattr(r, n, ref)
        layout(r)

    done = pl.pallas_call(
        layout_kernel,
        out_shape=[jax.ShapeDtypeStruct(*outs[n]) for n in outs],
        in_specs=[pl.BlockSpec(memory_space=pltpu.VMEM)] * len(names),
        out_specs=[pl.BlockSpec(memory_space=pltpu.VMEM)] * len(outs),
        compiler_params=pltpu.CompilerParams(vmem_limit_bytes=VMEM_LIMIT),
        name="layout",
    )(*[b[n] for n in names])
    return tuple(done[:10]) + (done[10].reshape(model),)


def solution(mesh):
    placed = (
        P(("tok", "ffn"), None),
        P(("tok", "ffn"), None),
        P(("tok", "ffn"), None),
        P("tok", None),
        P("tok", None),
        P(),
        P(),
        P(),
        P(None, None, "ffn"),
        P(None, "ffn", None),
        P(),
        P(),
    )
    return jax.shard_map(
        on_device,
        mesh=mesh,
        in_specs=placed,
        out_specs=(
            P(("tok", "ffn"), None),
            P(("tok", "ffn"), None),
            P(("tok", "ffn"), None),
            P(None, None, "tok", "ffn"),
            P(None, "tok", "ffn"),
            P(None, "ffn", "tok"),
            P(None, "tok", "ffn"),
            P(None, "ffn", "tok"),
            P(),
            P(),
            P(),
        ),
        check_vma=False,
    )
```
